32 devices in a mesh: cuts: 2 (over x), mode: 8 (over z, y), branch: 2 (over core).
Axes of the slice: x: 2, y: 2, z: 4, core: 2. Of those that a mesh axis runs over, the one named last changes fastest.
Arguments:
- leaves: bfloat16 [8, 2, 32, 512, 512], P('branch', None, ('cuts', 'mode')), parts along dimension 2, may hold values from -0.1875 to 0.1875
- join_order: int32 [7], replicated, may hold values from 0 to 1
- slice_values: int32 [32], P(('cuts', 'mode')), parts along dimension 0, may hold values from 0 to 1
- boundary: bfloat16 [2, 2, 512, 512], replicated, may hold values from -4 to 4
Outputs:
- amplitudes: float32 [2, 32, 512, 512], P(None, ('cuts', 'mode'), 'branch'), parts along dimension 1
The draws below stay inside these ranges and needn't reach their ends.
There are 2 independent parts, one for each index of `cuts`. The reference program is written for one: setup_inputs(seed, part) draws one part's arguments, and reference() takes and returns one part's arrays. A program takes and returns all parts, laid end to end along the dimension named above; an argument that names none is the same for every part. Nothing has to cross between parts.
Inputs may be any that keep to these rules, and one draw needn't show every extreme that they name: `join_order`: 1 puts the second operand of the join on the left.
All inputs are finite; a program needn't handle non-finite values.
Results may differ from the reference program's by a relative error of at most 0.0076.
Values may be sent and summed in bfloat16 or wider, within the bound.
No kernel may reach another device: no remote copies, remote signals or barrier semaphores. Data moves between devices by JAX's collectives and lax.ppermute only.
A program may use at most 64 MiB of HBM per device.

```python
import jax
import jax.numpy as jnp
from jax import lax

M = 512
LEAVES = 8
BOND = 2
BATCH = 16
N_MODE = 8


def with_ends(values, own_key, smallest, largest):
    extent = values.shape
    index_at = [jax.random.randint(jax.random.fold_in(own_key, axis), (), 0, extent[axis]) for axis in range(len(extent))]
    values = values.at[tuple(index_at)].set(smallest)
    longest = extent.index(max(extent))
    index_at[longest] = (index_at[longest] + 1) % extent[longest]
    return values.at[tuple(index_at)].set(largest)


def block_levels(own_key, extent, split, smallest, largest):
    def one(position, blocks):
        draws = jax.random.uniform(jax.random.fold_in(jax.random.fold_in(own_key, 6), position), (blocks,), jnp.float32, smallest / len(split), largest / len(split))
        return jnp.repeat(jnp.exp(draws), extent[position] // blocks).reshape((-1,) + (1,) * (len(extent) - position - 1))

    factor_of = one(*split[0])
    for cut in split[1:]:
        factor_of = factor_of * one(*cut)
    return factor_of


def bell_draw(own_key, shape, deviation, most, split=(), kind=jnp.bfloat16):
    array = deviation * jax.random.normal(own_key, shape, jnp.float32)
    if split:
        array = array * block_levels(own_key, shape, split, -0.22, 0.18)
    return jnp.clip(array, -most, most).astype(kind)


def setup_inputs(seed: int = 0, part: int = 0) -> dict:
    streams_of = jax.random.split(jax.random.key(seed), 5)
    own_keys = jax.random.split(jax.random.fold_in(streams_of[4], part), 5)
    leaves = bell_draw(own_keys[0], (LEAVES, 2, BATCH, M, M), (2 * M) ** -0.5, 0.1875, ((0, 2), (2, 8)))
    join_order = with_ends(jax.random.randint(streams_of[1], (LEAVES - 1,), 0, 2), jax.random.fold_in(streams_of[1], 1), 0, 1).astype(jnp.int32)
    slice_values = with_ends(jax.random.randint(own_keys[2], (BATCH,), 0, BOND), jax.random.fold_in(own_keys[2], 1), 0, BOND - 1).astype(jnp.int32)
    boundary = bell_draw(streams_of[3], (BOND, 2, M, M), 0.7, 4.0)
    return {"leaves": leaves, "join_order": join_order, "slice_values": slice_values, "boundary": boundary}


def complex_sums(left_op, right_op):
    spec = "bij,bjk->bik"
    left_real = left_op[0].astype(jnp.float32)
    left_imag = left_op[1].astype(jnp.float32)
    right_real = right_op[0].astype(jnp.float32)
    right_imag = right_op[1].astype(jnp.float32)
    real_part = jnp.einsum(spec, left_real, right_real) - jnp.einsum(spec, left_imag, right_imag)
    imag_part = jnp.einsum(spec, left_real, right_imag) + jnp.einsum(spec, left_imag, right_real)
    return jnp.stack([real_part, imag_part])


def complex_product(left_op, right_op):
    return complex_sums(left_op, right_op).astype(jnp.bfloat16)


def join_pair(left_op, right_op, swapped):
    return lax.cond(swapped == 1, lambda: complex_product(right_op, left_op), lambda: complex_product(left_op, right_op))


def reorder_rows(tensor):
    blocks = N_MODE
    block_rows = M // blocks
    viewed = tensor.reshape(2, BATCH, blocks, block_rows, M)
    return jnp.transpose(viewed, (0, 2, 1, 3, 4)).reshape(2, BATCH, M, M)


def reference(leaves, join_order, slice_values, boundary):
    first_level = []
    for index in range(4):
        joined = join_pair(leaves[2 * index], leaves[2 * index + 1], join_order[index])
        first_level.append(reorder_rows(joined))
    second_level = []
    for index in range(2):
        joined = join_pair(first_level[2 * index], first_level[2 * index + 1], join_order[4 + index])
        second_level.append(reorder_rows(joined))
    top_tensor = join_pair(second_level[0], second_level[1], join_order[6])
    chosen = jnp.where(slice_values[None, :, None, None] == 1, boundary[1][:, None], boundary[0][:, None])
    return complex_sums(top_tensor, chosen).astype(jnp.float32)
```

```python
import jax
import jax.numpy as jnp
from jax import lax
from jax.sharding import PartitionSpec as P


def from_partner(value, axis, bit):
    mask = 2**bit
    pairs = [(source, source ^ mask) for source in range(lax.axis_size(axis))]
    return lax.ppermute(value, axis, pairs)


def complex_sums(left_op, right_op):
    spec = "bij,bjk->bik"
    real_part = jnp.einsum(
        spec, left_op[0], right_op[0], preferred_element_type=jnp.float32
    ) - jnp.einsum(spec, left_op[1], right_op[1], preferred_element_type=jnp.float32)
    imag_part = jnp.einsum(
        spec, left_op[0], right_op[1], preferred_element_type=jnp.float32
    ) + jnp.einsum(spec, left_op[1], right_op[0], preferred_element_type=jnp.float32)
    return jnp.stack([real_part, imag_part])


def complex_product(left_op, right_op):
    return complex_sums(left_op, right_op).astype(jnp.bfloat16)


def join_pair(left_op, right_op, swapped):
    return lax.cond(
        swapped == 1,
        lambda: complex_product(right_op, left_op),
        lambda: complex_product(left_op, right_op),
    )


def split_rows(tensor, blocks):
    shape = tensor.shape
    return tensor.reshape(shape[0], shape[1], blocks, shape[2] // blocks, shape[3])


def grouped_exchange(tensor, groups):
    size = len(groups[0])
    shape = tensor.shape
    batch, width = shape[1], shape[3]
    viewed = tensor.reshape(shape[0], batch, size, batch, width // (size * batch), width)
    viewed = jnp.transpose(viewed, (2, 0, 3, 1, 4, 5))
    moved = lax.all_to_all(viewed, "mode", 0, 0, axis_index_groups=groups, tiled=True)
    return jnp.transpose(moved, (1, 2, 0, 3, 4, 5)).reshape(shape)


def full_exchange(tensor, halves):
    blocks = lax.axis_size("mode")
    shape = tensor.shape
    batch, width = shape[1], shape[3]
    moved = lax.all_to_all(split_rows(tensor, blocks), "mode", split_axis=2, concat_axis=1, tiled=True)
    moved = moved.reshape(shape[0], halves, blocks // halves, batch, width // blocks, width)
    return jnp.transpose(moved, (0, 2, 3, 1, 4, 5)).reshape(shape)


def per_device(leaves, join_order, slice_values, boundary):
    blocks = lax.axis_size("mode")
    halves = leaves.shape[2]
    size = blocks // halves
    groups = [[half * size + place for place in range(size)] for half in range(halves)]
    branch_index = lax.axis_index("branch")
    base_index = 2 * branch_index
    first_pair = join_pair(leaves[0], leaves[1], join_order[base_index])
    second_pair = join_pair(leaves[2], leaves[3], join_order[base_index + 1])
    first_pair = grouped_exchange(first_pair, groups)
    second_pair = grouped_exchange(second_pair, groups)
    middle = join_pair(first_pair, second_pair, join_order[4 + branch_index])
    middle = full_exchange(middle, halves)
    width = middle.shape[3]
    half_rows = width // 2
    chosen = jnp.where(
        slice_values[None, :, None, None] == 1, boundary[1][:, None], boundary[0][:, None]
    )
    top_order = join_order[-1]
    partner = from_partner(middle, "branch", 0)
    is_first = branch_index == 0
    upper = jnp.where(is_first, middle, partner)
    lower = jnp.where(is_first, partner, middle)
    leading = jnp.where(top_order == 1, lower, upper)
    trailing = jnp.where(top_order == 1, upper, lower)
    leading = lax.dynamic_slice_in_dim(leading, branch_index * half_rows, half_rows, 2)
    top_half = complex_product(leading, trailing)
    amplitudes = complex_sums(top_half, chosen)
    return amplitudes


def solution(mesh):
    in_specs = (P("branch", None, ("cuts", "mode"), None, None), P(), P(("cuts", "mode")), P())
    out_specs = P(None, ("cuts", "mode"), "branch", None)
    return jax.shard_map(
        per_device, mesh=mesh, in_specs=in_specs, out_specs=out_specs, check_vma=False
    )
```

```python
import functools

import jax
import jax.numpy as jnp
from jax import lax
from jax.experimental import pallas as pl
from jax.experimental.pallas import tpu as pltpu
from jax.sharding import PartitionSpec as P

HBM = pl.BlockSpec(memory_space=pl.ANY)
SMEM = pl.BlockSpec(memory_space=pltpu.SMEM)
VMEM_LIMIT = 40 * 2**20


def complex_dot(left_real, left_imag, right):
    left = jnp.concatenate(
        [
            jnp.concatenate([left_real, -left_imag], axis=1),
            jnp.concatenate([left_imag, left_real], axis=1),
        ],
        axis=0,
    )
    sums = jnp.dot(left, right, preferred_element_type=jnp.float32)
    rows = left_real.shape[0]
    return sums[:rows], sums[rows:]


class Copies:
    def __init__(self, sems):
        self.sems = sems
        self.used = 0

    def start(self, source, target):
        copy = pltpu.make_async_copy(source, target, self.sems.at[self.used])
        self.used += 1
        copy.start()
        return copy


def run_kernel(body, outs, scratch, copies, flops, operands, specs, aliases=None):
    moved = sum(x.size * x.dtype.itemsize for x in outs) + 2**21
    return pl.pallas_call(
        body,
        out_shape=outs,
        in_specs=specs,
        out_specs=[HBM] * len(outs),
        scratch_shapes=list(scratch) + [pltpu.SemaphoreType.DMA((copies,))],
        input_output_aliases=aliases or {},
        compiler_params=pltpu.CompilerParams(vmem_limit_bytes=VMEM_LIMIT),
        cost_estimate=pl.CostEstimate(flops=flops, bytes_accessed=moved, transcendentals=0),
    )(*operands)


class Plan:
    def __init__(self, leaves):
        self.modes = lax.axis_size("mode")
        self.batch = leaves.shape[2]
        self.width = leaves.shape[4]
        self.rows = self.width // self.modes
        self.size = self.modes // self.batch
        self.ways = self.batch
        self.places = self.size // self.ways
        assert self.batch == 2 and lax.axis_size("branch") == 2

    def mode_of(self, high, place, way):
        return (high * self.places + place) * self.ways + way

    def here(self):
        mode = lax.axis_index("mode")
        return mode // self.size, (mode % self.size) // self.ways, mode % self.ways


def first_level(plan, leaves, join_order, role, spans):
    width, batch, rows = plan.width, plan.batch, plan.rows
    lowest, highest = spans[0][0], spans[-1][1]
    total = highest - lowest
    half = width // plan.ways
    chunk_blocks = [(high - low) // rows for low, high in spans]

    def body(order, leaf, *rest):
        outs, (upper, lower, result, sems) = rest[: 2 * len(spans)], rest[2 * len(spans) :]
        copies = Copies(sems)
        branch = lax.axis_index("branch")
        _, _, way = plan.here()
        pair = jnp.where(order[2 * lax.axis_size("branch") + branch] == 1, 1 - role, role)
        swapped = jnp.where(order[2 * branch + pair] == 1, 1, 0)
        first, second = 2 * pair + swapped, 2 * pair + 1 - swapped
        loads = []
        for item in range(batch):
            mine = []
            for place in range(plan.ways):
                target = (way + place) % plan.ways
                mine.append(
                    copies.start(
                        leaf.at[first, :, item, pl.ds(target * half + lowest, total)],
                        upper.at[item, :, place],
                    )
                )
            mine.append(copies.start(leaf.at[second, :, item], lower.at[item]))
            loads.append(mine)
        stores = []
        for item in range(batch):
            for copy in loads[item]:
                copy.wait()
            parts = complex_dot(
                upper[item, 0].reshape(plan.ways * total, width),
                upper[item, 1].reshape(plan.ways * total, width),
                lower[item].reshape(2 * width, width),
            )
            for part in range(2):
                result[item, part] = (
                    parts[part].astype(jnp.bfloat16).reshape(plan.ways, total, width)
                )
            for place in range(plan.ways):
                for index, (low, high) in enumerate(spans):
                    for block in range(chunk_blocks[index]):
                        begin = low - lowest + block * rows
                        stores.append(
                            copies.start(
                                result.at[item, :, place, pl.ds(begin, rows)],
                                outs[2 * index + place].at[:, block, item],
                            )
                        )
        for copy in stores:
            copy.wait()

    outs = [
        jax.ShapeDtypeStruct((2, blocks, batch, rows, width), jnp.bfloat16)
        for blocks in chunk_blocks
        for _ in range(plan.ways)
    ]
    scratch = [
        pltpu.VMEM((batch, 2, plan.ways, total, width), jnp.bfloat16),
        pltpu.VMEM((batch, 2, width, width), jnp.bfloat16),
        pltpu.VMEM((batch, 2, plan.ways, total, width), jnp.bfloat16),
    ]
    copies = batch * (plan.ways + 1) + batch * plan.ways * sum(chunk_blocks)
    flops = 8 * batch * plan.ways * total * width * width
    results = run_kernel(body, outs, scratch, copies, flops, [join_order, leaves], [SMEM, HBM])
    return [results[2 * index : 2 * index + 2] for index in range(len(spans))]


def second_level(plan, left_own, left_way, right_own, right_way, right_places, right_both):
    width, batch, rows, ways, places = plan.width, plan.batch, plan.rows, plan.ways, plan.places
    blocks = left_own.shape[1]
    held = ways * batch * rows
    others = places - 1

    def body(*refs):
        sources = refs[: 4 + 2 * others]
        outs = refs[4 + 2 * others : 4 + 2 * others + ways * batch]
        left, right, result, sems = refs[4 + 2 * others + ways * batch :]
        copies = Copies(sems)
        branch = lax.axis_index("branch")
        high, place, way = plan.here()
        loads = [
            copies.start(sources[0], left.at[:, :, way]),
            copies.start(sources[1], left.at[:, :, 1 - way]),
            copies.start(sources[2], right.at[:, :, place, way]),
            copies.start(sources[3], right.at[:, :, place, 1 - way]),
        ]
        for step in range(1, places):
            other = place ^ step
            loads.append(copies.start(sources[3 + step], right.at[:, :, other, way]))
            loads.append(copies.start(sources[3 + others + step], right.at[:, :, other, 1 - way]))
        for copy in loads:
            copy.wait()
        steps = [(a, b) for a in range(ways) for b in range(batch)]
        stores = []
        for block in range(blocks):
            halves = [
                jnp.concatenate([left[part, block, high ^ a, branch ^ b] for a, b in steps], axis=0)
                for part in range(2)
            ]
            parts = complex_dot(
                halves[0],
                halves[1],
                jnp.concatenate(
                    [right[part, block].reshape(width, width) for part in range(2)], axis=0
                ),
            )
            for part in range(2):
                result[block, part] = (
                    parts[part].astype(jnp.bfloat16).reshape(ways * batch, rows, width)
                )
            for index in range(ways * batch):
                stores.append(copies.start(result.at[block, :, index], outs[index].at[:, block]))
        for copy in stores:
            copy.wait()

    outs = [jax.ShapeDtypeStruct((2, blocks, rows, width), jnp.bfloat16)] * (ways * batch)
    scratch = [
        pltpu.VMEM((2, blocks, ways, batch, rows, width), jnp.bfloat16),
        pltpu.VMEM((2, blocks, places, ways, batch, rows, width), jnp.bfloat16),
        pltpu.VMEM((blocks, 2, ways * batch, rows, width), jnp.bfloat16),
    ]
    copies = 4 + 2 * others + blocks * ways * batch
    operands = [left_own, left_way, right_own, right_way, *right_places, *right_both]
    flops = 8 * blocks * held * width * width
    return run_kernel(body, outs, scratch, copies, flops, operands, [HBM] * len(operands))


def load_operands(plan, copies, order, messages, chunk_blocks, scratch, keep):
    mode = lax.axis_index("mode")
    near, item = (mode // plan.batch) % plan.ways, mode % plan.batch
    top = jnp.where(order[order.shape[0] - 1] == 1, 1, 0)
    steps = [(a, b) for a in range(plan.ways) for b in range(plan.batch)]
    loads = []
    begin = 0
    for chunk, blocks in zip(messages, chunk_blocks):
        for (a, b), message in zip(steps, chunk):
            role = item ^ b ^ top
            loads.append(
                copies.start(message, scratch.at[role, :, pl.ds(begin, blocks), near ^ a])
            )
        begin += blocks
    return loads


def top_operands(plan, scratch, half):
    width = plan.width
    kept = plan.size // 2
    left = [
        scratch[0, part, pl.ds(half * kept, kept)].reshape(width // 2, width) for part in range(2)
    ]
    right = jnp.concatenate([scratch[1, part].reshape(width, width) for part in range(2)], axis=0)
    return left[0], left[1], right


def top_scratch(plan):
    return pltpu.VMEM((2, 2, plan.size, plan.batch, plan.rows, plan.width), jnp.bfloat16)


def top_for_other(plan, join_order, messages):
    flat = [message for chunk in messages for message in chunk]
    count = len(messages[0])
    chunk_blocks = [chunk[0].shape[1] for chunk in messages]
    half_shape = (2, plan.width // 2, plan.width)

    def body(order, *refs):
        sources, (out, operands, result, sems) = refs[: len(flat)], refs[len(flat) :]
        copies = Copies(sems)
        grouped = [sources[i : i + count] for i in range(0, len(flat), count)]
        for copy in load_operands(plan, copies, order, grouped, chunk_blocks, operands, None):
            copy.wait()
        parts = complex_dot(*top_operands(plan, operands, 1 - lax.axis_index("branch")))
        for part in range(2):
            result[part] = parts[part].astype(jnp.bfloat16)
        copies.start(result, out).wait()

    flops = 4 * plan.width**3
    return run_kernel(
        body,
        [jax.ShapeDtypeStruct(half_shape, jnp.bfloat16)],
        [top_scratch(plan), pltpu.VMEM(half_shape, jnp.bfloat16)],
        len(flat) + 1,
        flops,
        [join_order, *flat],
        [SMEM] + [HBM] * len(flat),
    )[0]


def own_amplitudes(plan, join_order, slice_values, boundary, messages):
    flat = [message for chunk in messages for message in chunk]
    count = len(messages[0])
    chunk_blocks = [chunk[0].shape[1] for chunk in messages]
    width = plan.width

    def body(order, values, bound, *refs):
        sources, (out, operands, chosen, result, sems) = refs[: len(flat)], refs[len(flat) :]
        copies = Copies(sems)
        core = lax.axis_index("branch")
        grouped = [sources[i : i + count] for i in range(0, len(flat), count)]
        loads = load_operands(plan, copies, order, grouped, chunk_blocks, operands, None)
        value = jnp.where(values[core] == 1, 1, 0)
        late = copies.start(bound.at[value], chosen)
        for copy in loads:
            copy.wait()
        top = complex_dot(*top_operands(plan, operands, core))
        late.wait()
        parts = complex_dot(
            top[0].astype(jnp.bfloat16),
            top[1].astype(jnp.bfloat16),
            chosen[...].reshape(2 * width, width),
        )
        for part in range(2):
            result[part] = parts[part]
        copies.start(result, out.at[:, core]).wait()

    flops = 8 * plan.width**3
    return run_kernel(
        body,
        [jax.ShapeDtypeStruct((2, plan.batch, width // 2, width), jnp.float32)],
        [
            top_scratch(plan),
            pltpu.VMEM((2, width, width), jnp.bfloat16),
            pltpu.VMEM((2, width // 2, width), jnp.float32),
        ],
        len(flat) + 2,
        flops,
        [join_order, slice_values, boundary, *flat],
        [SMEM, SMEM, HBM] + [HBM] * len(flat),
    )[0]


def other_amplitudes(plan, slice_values, boundary, top, amplitudes):
    width = plan.width

    def body(values, bound, top, _, out, left, chosen, result, sems):
        copies = Copies(sems)
        other = 1 - lax.axis_index("branch")
        value = jnp.where(values[other] == 1, 1, 0)
        loads = [copies.start(top, left), copies.start(bound.at[value], chosen)]
        for copy in loads:
            copy.wait()
        parts = complex_dot(left[0], left[1], chosen[...].reshape(2 * width, width))
        for part in range(2):
            result[part] = parts[part]
        copies.start(result, out.at[:, other]).wait()

    return run_kernel(
        body,
        [jax.ShapeDtypeStruct(amplitudes.shape, jnp.float32)],
        [
            pltpu.VMEM((2, width // 2, width), jnp.bfloat16),
            pltpu.VMEM((2, width, width), jnp.bfloat16),
            pltpu.VMEM((2, width // 2, width), jnp.float32),
        ],
        3,
        4 * width**3,
        [slice_values, boundary, top, amplitudes],
        [SMEM, HBM, HBM, HBM],
        {3: 0},
    )[0]


def per_device(leaves, join_order, slice_values, boundary):
    plan = Plan(leaves)
    modes, ways, places, batch = plan.modes, plan.ways, plan.places, plan.batch
    every = [
        (high, place, way)
        for high in range(batch)
        for place in range(places)
        for way in range(ways)
    ]
    over_ways = [(plan.mode_of(h, p, w), plan.mode_of(h, p, w ^ 1)) for h, p, w in every]

    def over_places(step):
        return [(plan.mode_of(h, p, w), plan.mode_of(h, p ^ step, w)) for h, p, w in every]

    def to_rows(a, b):
        pairs = []
        for h, p, w in every:
            for k in range(2):
                target = (p * ways + (h ^ a)) * batch + (k ^ b)
                pairs.append((plan.mode_of(h, p, w) * 2 + k, target * 2 + w))
        return pairs

    quarter = plan.width // ways // 4
    spans = [(0, 2 * quarter), (2 * quarter, 3 * quarter), (3 * quarter, 4 * quarter)]
    groups = [[0], [1, 2]]
    left, right = {}, {}
    for group in groups:
        right.update(
            zip(group, first_level(plan, leaves, join_order, 1, [spans[c] for c in group]))
        )
        left.update(
            zip(group, first_level(plan, leaves, join_order, 0, [spans[c] for c in group]))
        )
    messages = []
    for chunk in range(len(spans)):
        right_own, right_send = right[chunk]
        left_own, left_send = left[chunk]
        right_way = lax.ppermute(right_send, "mode", over_ways)
        left_way = lax.ppermute(left_send, "mode", over_ways)
        right_places = [
            lax.ppermute(right_own, "mode", over_places(s)) for s in range(1, places)
        ]
        right_both = [lax.ppermute(right_way, "mode", over_places(s)) for s in range(1, places)]
        rows = second_level(
            plan, left_own, left_way, right_own, right_way, right_places, right_both
        )
        messages.append(
            [
                lax.ppermute(rows[a * batch + b], ("mode", "branch"), to_rows(a, b))
                for a in range(ways)
                for b in range(batch)
            ]
        )
    top_other = top_for_other(plan, join_order, messages)
    top_received = lax.ppermute(top_other, "branch", [(0, 1), (1, 0)])
    amplitudes = own_amplitudes(plan, join_order, slice_values, boundary, messages)
    return other_amplitudes(plan, slice_values, boundary, top_received, amplitudes)


def solution(mesh):
    in_specs = (P("branch", None, ("cuts", "mode"), None, None), P(), P(("cuts", "mode")), P())
    out_specs = P(None, ("cuts", "mode"), "branch", None)
    return jax.shard_map(
        per_device, mesh=mesh, in_specs=in_specs, out_specs=out_specs, check_vma=False
    )
```

```python
import functools

import jax
import jax.numpy as jnp
from jax import lax
from jax.experimental import pallas as pl
from jax.experimental.pallas import tpu as pltpu
from jax.sharding import PartitionSpec as P

ANY = pl.BlockSpec(memory_space=pl.ANY)
SMEM = pl.BlockSpec(memory_space=pltpu.SMEM)
VMEM_LIMIT = 40 * 2**20
VMEM_MOST = 60 * 2**20


def complex_dot(left_real, left_imag, right):
    left = jnp.concatenate(
        [
            jnp.concatenate([left_real, -left_imag], axis=1),
            jnp.concatenate([left_imag, left_real], axis=1),
        ],
        axis=0,
    )
    sums = jnp.dot(left, right, preferred_element_type=jnp.float32)
    rows = left_real.shape[0]
    return sums[:rows], sums[rows:]


class Copies:
    def __init__(self, sems):
        self.sems = sems
        self.used = 0

    def start(self, source, target):
        copy = pltpu.make_async_copy(source, target, self.sems.at[self.used])
        self.used += 1
        copy.start()
        return copy


def run_kernel(body, outs, scratch, copies, flops, operands, specs, aliases=None, limit=VMEM_LIMIT):
    moved = sum(x.size * x.dtype.itemsize for x in outs) + 2**21
    return pl.pallas_call(
        body,
        out_shape=outs,
        in_specs=specs,
        out_specs=[ANY] * len(outs),
        scratch_shapes=list(scratch) + [pltpu.SemaphoreType.DMA((copies,))],
        input_output_aliases=aliases or {},
        compiler_params=pltpu.CompilerParams(vmem_limit_bytes=limit),
        cost_estimate=pl.CostEstimate(flops=flops, bytes_accessed=moved, transcendentals=0),
    )(*operands)


class Plan:
    def __init__(self, leaves):
        self.modes = lax.axis_size("mode")
        self.batch = leaves.shape[2]
        self.width = leaves.shape[4]
        self.rows = self.width // self.modes
        self.size = self.modes // self.batch
        self.ways = self.batch
        self.places = self.size // self.ways
        assert self.batch == 2 and lax.axis_size("branch") == 2

    def mode_of(self, high, place, way):
        return (high * self.places + place) * self.ways + way

    def here(self):
        mode = lax.axis_index("mode")
        return mode // self.size, (mode % self.size) // self.ways, mode % self.ways


def first_level(plan, leaves, join_order, role, parts, limit):
    width, batch, rows, ways = plan.width, plan.batch, plan.rows, plan.ways
    half = width // ways

    def body(order, leaf, *rest):
        outs, (upper, lower, result, sems) = rest[:-4], rest[-4:]
        copies = Copies(sems)
        branch = lax.axis_index("branch")
        _, _, way = plan.here()
        pair = jnp.where(order[2 * lax.axis_size("branch") + branch] == 1, 1 - role, role)
        swapped = jnp.where(order[2 * branch + pair] == 1, 1, 0)
        first, second = 2 * pair + swapped, 2 * pair + 1 - swapped
        loads = [
            [
                copies.start(leaf.at[second, :, item], lower.at[item]),
                copies.start(leaf.at[first, :, item], upper.at[item]),
            ]
            for item in range(batch)
        ]
        stores = []
        for item in range(batch):
            for copy in loads[item]:
                copy.wait()
            sums = complex_dot(
                upper[item, 0], upper[item, 1], lower[item].reshape(2 * width, width)
            )
            for part in range(2):
                result[item, part] = sums[part].astype(jnp.bfloat16)
            for side, target in enumerate((way, 1 - way)):
                begin = 0
                for chunk, blocks in enumerate(parts):
                    for block in range(blocks):
                        source = result.at[item, :, pl.ds(target * half + begin, rows)]
                        place = outs[2 * chunk + side].at[:, block, item]
                        stores.append(copies.start(source, place))
                        begin += rows
        for copy in stores:
            copy.wait()

    outs = [
        jax.ShapeDtypeStruct((2, blocks, batch, rows, width), jnp.bfloat16)
        for blocks in parts
        for _ in range(ways)
    ]
    scratch = [pltpu.VMEM((batch, 2, width, width), jnp.bfloat16) for _ in range(3)]
    copies = 2 * batch + batch * ways * sum(parts)
    flops = 8 * batch * width**3
    results = run_kernel(
        body, outs, scratch, copies, flops, [join_order, leaves], [SMEM, ANY], limit=limit
    )
    return [results[2 * index : 2 * index + 2] for index in range(len(parts))]


def once_arrived(value, after):
    def body(*refs):
        pass

    return pl.pallas_call(
        body,
        out_shape=jax.ShapeDtypeStruct(value.shape, value.dtype),
        in_specs=[ANY] * (1 + len(after)),
        out_specs=ANY,
        input_output_aliases={0: 0},
    )(value, *after)


def second_level(plan, blocks, operands, pick):
    width, batch, rows, ways, places = plan.width, plan.batch, plan.rows, plan.ways, plan.places
    held = ways * batch * rows

    def body(*refs):
        left_kept, left_sent, right_kept, right_sent, others = pick(refs[: len(operands)])
        rest = refs[len(operands) :]
        outs, (left, right, result, sems) = rest[:-4], rest[-4:]
        copies = Copies(sems)
        branch = lax.axis_index("branch")
        high, place, way = plan.here()
        loads = [
            copies.start(left_kept, left.at[:, :, way]),
            copies.start(left_sent, left.at[:, :, 1 - way]),
            copies.start(right_kept, right.at[:, :, place, way]),
            copies.start(right_sent, right.at[:, :, place, 1 - way]),
        ]
        for step, (kept, sent) in enumerate(others):
            other = place ^ (step + 1)
            loads.append(copies.start(kept, right.at[:, :, other, way]))
            loads.append(copies.start(sent, right.at[:, :, other, 1 - way]))
        for copy in loads:
            copy.wait()
        steps = [(a, b) for a in range(ways) for b in range(batch)]
        stores = []
        for block in range(blocks):
            halves = [
                jnp.concatenate([left[part, block, high ^ a, branch ^ b] for a, b in steps], axis=0)
                for part in range(2)
            ]
            parts = complex_dot(
                halves[0],
                halves[1],
                jnp.concatenate(
                    [right[part, block].reshape(width, width) for part in range(2)], axis=0
                ),
            )
            for part in range(2):
                result[block, part] = (
                    parts[part].astype(jnp.bfloat16).reshape(ways * batch, rows, width)
                )
            for index in range(ways * batch):
                stores.append(copies.start(result.at[block, :, index], outs[index].at[:, block]))
        for copy in stores:
            copy.wait()

    outs = [jax.ShapeDtypeStruct((2, blocks, rows, width), jnp.bfloat16)] * (ways * batch)
    scratch = [
        pltpu.VMEM((2, blocks, ways, batch, rows, width), jnp.bfloat16),
        pltpu.VMEM((2, blocks, places, ways, batch, rows, width), jnp.bfloat16),
        pltpu.VMEM((blocks, 2, ways * batch, rows, width), jnp.bfloat16),
    ]
    copies = 4 + 2 * (places - 1) + blocks * ways * batch
    flops = 8 * blocks * held * width * width
    return run_kernel(body, outs, scratch, copies, flops, operands, [ANY] * len(operands))


def load_operands(plan, copies, order, messages, chunk_blocks, scratch, keep):
    mode = lax.axis_index("mode")
    near, item = (mode // plan.batch) % plan.ways, mode % plan.batch
    top = jnp.where(order[order.shape[0] - 1] == 1, 1, 0)
    steps = [(a, b) for a in range(plan.ways) for b in range(plan.batch)]
    loads = []
    begin = 0
    for chunk, blocks in zip(messages, chunk_blocks):
        for (a, b), message in zip(steps, chunk):
            role = item ^ b ^ top
            loads.append(
                copies.start(message, scratch.at[role, :, pl.ds(begin, blocks), near ^ a])
            )
        begin += blocks
    return loads


def top_operands(plan, scratch, half):
    width = plan.width
    kept = plan.size // 2
    left = [
        scratch[0, part, pl.ds(half * kept, kept)].reshape(width // 2, width) for part in range(2)
    ]
    right = jnp.concatenate([scratch[1, part].reshape(width, width) for part in range(2)], axis=0)
    return left[0], left[1], right


def top_scratch(plan):
    return pltpu.VMEM((2, 2, plan.size, plan.batch, plan.rows, plan.width), jnp.bfloat16)


def top_for_other(plan, join_order, messages):
    flat = [message for chunk in messages for message in chunk]
    count = len(messages[0])
    chunk_blocks = [chunk[0].shape[1] for chunk in messages]
    half_shape = (2, plan.width // 2, plan.width)

    def body(order, *refs):
        sources, (out, operands, result, sems) = refs[: len(flat)], refs[len(flat) :]
        copies = Copies(sems)
        grouped = [sources[i : i + count] for i in range(0, len(flat), count)]
        for copy in load_operands(plan, copies, order, grouped, chunk_blocks, operands, None):
            copy.wait()
        parts = complex_dot(*top_operands(plan, operands, 1 - lax.axis_index("branch")))
        for part in range(2):
            result[part] = parts[part].astype(jnp.bfloat16)
        copies.start(result, out).wait()

    flops = 4 * plan.width**3
    return run_kernel(
        body,
        [jax.ShapeDtypeStruct(half_shape, jnp.bfloat16)],
        [top_scratch(plan), pltpu.VMEM(half_shape, jnp.bfloat16)],
        len(flat) + 1,
        flops,
        [join_order, *flat],
        [SMEM] + [ANY] * len(flat),
    )[0]


def own_amplitudes(plan, join_order, slice_values, boundary, messages):
    flat = [message for chunk in messages for message in chunk]
    count = len(messages[0])
    chunk_blocks = [chunk[0].shape[1] for chunk in messages]
    width = plan.width

    def body(order, values, bound, *refs):
        sources, (out, operands, chosen, result, sems) = refs[: len(flat)], refs[len(flat) :]
        copies = Copies(sems)
        core = lax.axis_index("branch")
        grouped = [sources[i : i + count] for i in range(0, len(flat), count)]
        loads = load_operands(plan, copies, order, grouped, chunk_blocks, operands, None)
        value = jnp.where(values[core] == 1, 1, 0)
        late = copies.start(bound.at[value], chosen)
        for copy in loads:
            copy.wait()
        top = complex_dot(*top_operands(plan, operands, core))
        late.wait()
        parts = complex_dot(
            top[0].astype(jnp.bfloat16),
            top[1].astype(jnp.bfloat16),
            chosen[...].reshape(2 * width, width),
        )
        for part in range(2):
            result[part] = parts[part]
        copies.start(result, out.at[:, core]).wait()

    flops = 8 * plan.width**3
    return run_kernel(
        body,
        [jax.ShapeDtypeStruct((2, plan.batch, width // 2, width), jnp.float32)],
        [
            top_scratch(plan),
            pltpu.VMEM((2, width, width), jnp.bfloat16),
            pltpu.VMEM((2, width // 2, width), jnp.float32),
        ],
        len(flat) + 2,
        flops,
        [join_order, slice_values, boundary, *flat],
        [SMEM, SMEM, ANY] + [ANY] * len(flat),
    )[0]


def other_amplitudes(plan, slice_values, boundary, top, amplitudes):
    width = plan.width

    def body(values, bound, top, _, out, left, chosen, result, sems):
        copies = Copies(sems)
        other = 1 - lax.axis_index("branch")
        value = jnp.where(values[other] == 1, 1, 0)
        loads = [copies.start(top, left), copies.start(bound.at[value], chosen)]
        for copy in loads:
            copy.wait()
        parts = complex_dot(left[0], left[1], chosen[...].reshape(2 * width, width))
        for part in range(2):
            result[part] = parts[part]
        copies.start(result, out.at[:, other]).wait()

    return run_kernel(
        body,
        [jax.ShapeDtypeStruct(amplitudes.shape, jnp.float32)],
        [
            pltpu.VMEM((2, width // 2, width), jnp.bfloat16),
            pltpu.VMEM((2, width, width), jnp.bfloat16),
            pltpu.VMEM((2, width // 2, width), jnp.float32),
        ],
        3,
        4 * width**3,
        [slice_values, boundary, top, amplitudes],
        [SMEM, ANY, ANY, ANY],
        {3: 0},
    )[0]


def per_device(leaves, join_order, slice_values, boundary):
    plan = Plan(leaves)
    modes, ways, places, batch = plan.modes, plan.ways, plan.places, plan.batch
    every = [
        (high, place, way)
        for high in range(batch)
        for place in range(places)
        for way in range(ways)
    ]
    over_ways = [(plan.mode_of(h, p, w), plan.mode_of(h, p, w ^ 1)) for h, p, w in every]

    def over_places(step):
        return [(plan.mode_of(h, p, w), plan.mode_of(h, p ^ step, w)) for h, p, w in every]

    def to_rows(a, b):
        pairs = []
        for h, p, w in every:
            for k in range(2):
                target = (p * ways + (h ^ a)) * batch + (k ^ b)
                pairs.append((plan.mode_of(h, p, w) * 2 + k, target * 2 + w))
        return pairs

    parts = [plan.size // 2] * 2
    right = first_level(plan, leaves, join_order, 1, parts, VMEM_MOST)
    left = first_level(plan, leaves, join_order, 0, parts, VMEM_LIMIT)
    others = range(1, places)
    steps = [(a, b) for a in range(ways) for b in range(batch)]
    messages = []
    order = list(range(len(steps)))[::-1]
    arrived = []
    for chunk, blocks in enumerate(parts):
        right_kept, right_sent = right[chunk]
        left_kept, left_sent = left[chunk]
        right_sent = lax.ppermute(right_sent, "mode", over_ways)
        kept_there = [lax.ppermute(right_kept, "mode", over_places(step)) for step in others]
        left_sent = lax.ppermute(left_sent, "mode", over_ways)
        sent_there = [lax.ppermute(right_sent, "mode", over_places(step)) for step in others]
        operands = [
            left_kept,
            left_sent,
            right_kept,
            right_sent,
            *kept_there,
            *sent_there,
            *arrived[:3],
        ]

        def pick(refs):
            there = refs[4 : 2 + 2 * places]
            pairs = list(zip(there[: places - 1], there[places - 1 :]))
            return refs[0], refs[1], refs[2], refs[3], pairs

        rows = second_level(plan, blocks, operands, pick)
        arrived = [
            lax.ppermute(rows[i], ("mode", "branch"), to_rows(*steps[i])) for i in order
        ]
        messages.append(arrived[::-1])
    top_other = top_for_other(plan, join_order, messages)
    top_received = lax.ppermute(top_other, "branch", [(0, 1), (1, 0)])
    amplitudes = own_amplitudes(plan, join_order, slice_values, boundary, messages)
    return other_amplitudes(plan, slice_values, boundary, top_received, amplitudes)


def solution(mesh):
    in_specs = (P("branch", None, ("cuts", "mode"), None, None), P(), P(("cuts", "mode")), P())
    out_specs = P(None, ("cuts", "mode"), "branch", None)
    return jax.shard_map(
        per_device, mesh=mesh, in_specs=in_specs, out_specs=out_specs, check_vma=False
    )
```

```python
import functools

import jax
import jax.numpy as jnp
from jax import lax
from jax.experimental import pallas as pl
from jax.experimental.pallas import tpu as pltpu
from jax.sharding import PartitionSpec as P

ANY = pl.BlockSpec(memory_space=pl.ANY)
SMEM = pl.BlockSpec(memory_space=pltpu.SMEM)
VMEM_LIMIT = 40 * 2**20
VMEM_MOST = 60 * 2**20


def complex_dot(left_real, left_imag, right):
    left = jnp.concatenate(
        [
            jnp.concatenate([left_real, -left_imag], axis=1),
            jnp.concatenate([left_imag, left_real], axis=1),
        ],
        axis=0,
    )
    sums = jnp.dot(left, right, preferred_element_type=jnp.float32)
    rows = left_real.shape[0]
    return sums[:rows], sums[rows:]


class Copies:
    def __init__(self, sems):
        self.sems = sems
        self.used = 0

    def start(self, source, target):
        copy = pltpu.make_async_copy(source, target, self.sems.at[self.used])
        self.used += 1
        copy.start()
        return copy


def run_kernel(body, outs, scratch, copies, flops, operands, specs, aliases=None, limit=VMEM_LIMIT):
    moved = sum(x.size * x.dtype.itemsize for x in outs) + 2**21
    return pl.pallas_call(
        body,
        out_shape=outs,
        in_specs=specs,
        out_specs=[ANY] * len(outs),
        scratch_shapes=list(scratch) + [pltpu.SemaphoreType.DMA((copies,))],
        input_output_aliases=aliases or {},
        compiler_params=pltpu.CompilerParams(vmem_limit_bytes=limit),
        cost_estimate=pl.CostEstimate(flops=flops, bytes_accessed=moved, transcendentals=0),
    )(*operands)


class Plan:
    def __init__(self, leaves):
        self.modes = lax.axis_size("mode")
        self.batch = leaves.shape[2]
        self.width = leaves.shape[4]
        self.rows = self.width // self.modes
        self.size = self.modes // self.batch
        self.ways = self.batch
        self.places = self.size // self.ways
        assert self.batch == 2 and lax.axis_size("branch") == 2
        self.steps = [(1, 1), (1, 0), (0, 1), (0, 0)]

    def mode_of(self, high, place, way):
        return (high * self.places + place) * self.ways + way

    def here(self):
        mode = lax.axis_index("mode")
        return mode // self.size, (mode % self.size) // self.ways, mode % self.ways


def first_level(plan, leaves, join_order, jobs, limit):
    width, batch, rows, ways = plan.width, plan.batch, plan.rows, plan.ways
    half = width // ways
    chunks = [blocks for _, _, parts in jobs for blocks in parts]
    totals = [sum(parts) * rows for _, _, parts in jobs]

    def body(order, leaf, *rest):
        outs, rest = rest[: 2 * len(chunks)], rest[2 * len(chunks) :]
        copies = Copies(rest[-1])
        branch = lax.axis_index("branch")
        _, _, way = plan.here()
        loads = []
        for index, (role, begin, parts) in enumerate(jobs):
            upper, lower, _ = rest[3 * index : 3 * index + 3]
            pair = jnp.where(order[2 * lax.axis_size("branch") + branch] == 1, 1 - role, role)
            swapped = jnp.where(order[2 * branch + pair] == 1, 1, 0)
            first, second = 2 * pair + swapped, 2 * pair + 1 - swapped
            for item in range(batch):
                mine = [copies.start(leaf.at[second, :, item], lower.at[item])]
                for side, target in enumerate((way, 1 - way)):
                    span = pl.ds(target * half + begin * rows, totals[index])
                    source = leaf.at[first, :, item, span]
                    mine.append(copies.start(source, upper.at[item, :, side]))
                loads.append(mine)
        stores = []
        given = 0
        for index, (role, begin, parts) in enumerate(jobs):
            upper, lower, result = rest[3 * index : 3 * index + 3]
            total = totals[index]
            for item in range(batch):
                for copy in loads[index * batch + item]:
                    copy.wait()
                sums = complex_dot(
                    upper[item, 0].reshape(ways * total, width),
                    upper[item, 1].reshape(ways * total, width),
                    lower[item].reshape(2 * width, width),
                )
                for part in range(2):
                    result[item, part] = (
                        sums[part].astype(jnp.bfloat16).reshape(ways, total, width)
                    )
                for side in range(ways):
                    done = 0
                    for chunk, blocks in enumerate(parts):
                        for block in range(blocks):
                            source = result.at[item, :, side, pl.ds(done, rows)]
                            place = outs[2 * (given + chunk) + side].at[:, block, item]
                            stores.append(copies.start(source, place))
                            done += rows
            given += len(parts)
        for copy in stores:
            copy.wait()

    outs = [
        jax.ShapeDtypeStruct((2, blocks, batch, rows, width), jnp.bfloat16)
        for blocks in chunks
        for _ in range(ways)
    ]
    scratch = []
    for total in totals:
        scratch += [
            pltpu.VMEM((batch, 2, ways, total, width), jnp.bfloat16),
            pltpu.VMEM((batch, 2, width, width), jnp.bfloat16),
            pltpu.VMEM((batch, 2, ways, total, width), jnp.bfloat16),
        ]
    copies = len(jobs) * batch * (1 + ways) + batch * ways * sum(chunks)
    flops = 8 * batch * ways * sum(totals) * width**2
    results = run_kernel(
        body, outs, scratch, copies, flops, [join_order, leaves], [SMEM, ANY], limit=limit
    )
    return [results[2 * index : 2 * index + 2] for index in range(len(chunks))]


def second_level(plan, blocks, operands, pick):
    width, batch, rows, ways, places = plan.width, plan.batch, plan.rows, plan.ways, plan.places
    held = ways * batch * rows

    def body(*refs):
        left_kept, left_sent, right_kept, right_sent, others = pick(refs[: len(operands)])
        rest = refs[len(operands) :]
        outs, (left, right, result, sems) = rest[:-4], rest[-4:]
        copies = Copies(sems)
        branch = lax.axis_index("branch")
        high, place, way = plan.here()
        loads = [
            copies.start(left_kept, left.at[:, :, way]),
            copies.start(left_sent, left.at[:, :, 1 - way]),
            copies.start(right_kept, right.at[:, :, place, way]),
            copies.start(right_sent, right.at[:, :, place, 1 - way]),
        ]
        for step, (kept, sent) in enumerate(others):
            other = place ^ (step + 1)
            loads.append(copies.start(kept, right.at[:, :, other, way]))
            loads.append(copies.start(sent, right.at[:, :, other, 1 - way]))
        for copy in loads:
            copy.wait()
        stores = []
        for block in range(blocks):
            halves = [
                jnp.concatenate([left[part, block, high ^ a, branch ^ b] for a, b in plan.steps], axis=0)
                for part in range(2)
            ]
            parts = complex_dot(
                halves[0],
                halves[1],
                jnp.concatenate(
                    [right[part, block].reshape(width, width) for part in range(2)], axis=0
                ),
            )
            for part in range(2):
                result[block, part] = (
                    parts[part].astype(jnp.bfloat16).reshape(ways * batch, rows, width)
                )
            for index in range(ways * batch):
                stores.append(copies.start(result.at[block, :, index], outs[index].at[:, block]))
        for copy in stores:
            copy.wait()

    outs = [jax.ShapeDtypeStruct((2, blocks, rows, width), jnp.bfloat16)] * (ways * batch)
    scratch = [
        pltpu.VMEM((2, blocks, ways, batch, rows, width), jnp.bfloat16),
        pltpu.VMEM((2, blocks, places, ways, batch, rows, width), jnp.bfloat16),
        pltpu.VMEM((blocks, 2, ways * batch, rows, width), jnp.bfloat16),
    ]
    copies = 4 + 2 * (places - 1) + blocks * ways * batch
    flops = 8 * blocks * held * width * width
    return run_kernel(body, outs, scratch, copies, flops, operands, [ANY] * len(operands))


def load_operands(plan, copies, order, messages, chunk_blocks, scratch):
    mode = lax.axis_index("mode")
    near, item = (mode // plan.batch) % plan.ways, mode % plan.batch
    top = jnp.where(order[order.shape[0] - 1] == 1, 1, 0)
    loads = []
    begin = 0
    for chunk, blocks in zip(messages, chunk_blocks):
        for (a, b), message in zip(plan.steps, chunk):
            role = item ^ b ^ top
            loads.append(
                copies.start(message, scratch.at[role, :, pl.ds(begin, blocks), near ^ a])
            )
        begin += blocks
    return loads


def top_operands(plan, scratch, half):
    width = plan.width
    kept = plan.size // 2
    left = [
        scratch[0, part, pl.ds(half * kept, kept)].reshape(width // 2, width) for part in range(2)
    ]
    right = jnp.concatenate([scratch[1, part].reshape(width, width) for part in range(2)], axis=0)
    return left[0], left[1], right


def top_scratch(plan):
    return pltpu.VMEM((2, 2, plan.size, plan.batch, plan.rows, plan.width), jnp.bfloat16)


def top_for_other(plan, join_order, messages):
    flat = [message for chunk in messages for message in chunk]
    count = len(messages[0])
    chunk_blocks = [chunk[0].shape[1] for chunk in messages]
    half_shape = (2, plan.width // 2, plan.width)

    def body(order, *refs):
        sources, (out, operands, result, sems) = refs[: len(flat)], refs[len(flat) :]
        copies = Copies(sems)
        grouped = [sources[i : i + count] for i in range(0, len(flat), count)]
        for copy in load_operands(plan, copies, order, grouped, chunk_blocks, operands):
            copy.wait()
        parts = complex_dot(*top_operands(plan, operands, 1 - lax.axis_index("branch")))
        for part in range(2):
            result[part] = parts[part].astype(jnp.bfloat16)
        copies.start(result, out).wait()

    flops = 4 * plan.width**3
    return run_kernel(
        body,
        [jax.ShapeDtypeStruct(half_shape, jnp.bfloat16)],
        [top_scratch(plan), pltpu.VMEM(half_shape, jnp.bfloat16)],
        len(flat) + 1,
        flops,
        [join_order, *flat],
        [SMEM] + [ANY] * len(flat),
    )[0]


def own_amplitudes(plan, join_order, slice_values, boundary, messages):
    flat = [message for chunk in messages for message in chunk]
    count = len(messages[0])
    chunk_blocks = [chunk[0].shape[1] for chunk in messages]
    width = plan.width

    def body(order, values, bound, *refs):
        sources, (out, operands, chosen, result, sems) = refs[: len(flat)], refs[len(flat) :]
        copies = Copies(sems)
        core = lax.axis_index("branch")
        grouped = [sources[i : i + count] for i in range(0, len(flat), count)]
        loads = load_operands(plan, copies, order, grouped, chunk_blocks, operands)
        value = jnp.where(values[core] == 1, 1, 0)
        late = copies.start(bound.at[value], chosen)
        for copy in loads:
            copy.wait()
        top = complex_dot(*top_operands(plan, operands, core))
        late.wait()
        parts = complex_dot(
            top[0].astype(jnp.bfloat16),
            top[1].astype(jnp.bfloat16),
            chosen[...].reshape(2 * width, width),
        )
        for part in range(2):
            result[part] = parts[part]
        copies.start(result, out.at[:, core]).wait()

    flops = 8 * plan.width**3
    return run_kernel(
        body,
        [jax.ShapeDtypeStruct((2, plan.batch, width // 2, width), jnp.float32)],
        [
            top_scratch(plan),
            pltpu.VMEM((2, width, width), jnp.bfloat16),
            pltpu.VMEM((2, width // 2, width), jnp.float32),
        ],
        len(flat) + 2,
        flops,
        [join_order, slice_values, boundary, *flat],
        [SMEM, SMEM, ANY] + [ANY] * len(flat),
    )[0]


def other_amplitudes(plan, slice_values, boundary, top, amplitudes):
    width = plan.width

    def body(values, bound, top, _, out, left, chosen, result, sems):
        copies = Copies(sems)
        other = 1 - lax.axis_index("branch")
        value = jnp.where(values[other] == 1, 1, 0)
        loads = [copies.start(top, left), copies.start(bound.at[value], chosen)]
        for copy in loads:
            copy.wait()
        parts = complex_dot(left[0], left[1], chosen[...].reshape(2 * width, width))
        for part in range(2):
            result[part] = parts[part]
        copies.start(result, out.at[:, other]).wait()

    return run_kernel(
        body,
        [jax.ShapeDtypeStruct(amplitudes.shape, jnp.float32)],
        [
            pltpu.VMEM((2, width // 2, width), jnp.bfloat16),
            pltpu.VMEM((2, width, width), jnp.bfloat16),
            pltpu.VMEM((2, width // 2, width), jnp.float32),
        ],
        3,
        4 * width**3,
        [slice_values, boundary, top, amplitudes],
        [SMEM, ANY, ANY, ANY],
        {3: 0},
    )[0]


def per_device(leaves, join_order, slice_values, boundary):
    plan = Plan(leaves)
    modes, ways, places, batch = plan.modes, plan.ways, plan.places, plan.batch
    every = [
        (high, place, way)
        for high in range(batch)
        for place in range(places)
        for way in range(ways)
    ]
    over_ways = [(plan.mode_of(h, p, w), plan.mode_of(h, p, w ^ 1)) for h, p, w in every]

    def over_places(step):
        return [(plan.mode_of(h, p, w), plan.mode_of(h, p ^ step, w)) for h, p, w in every]

    def to_rows(a, b):
        pairs = []
        for h, p, w in every:
            for k in range(2):
                target = (p * ways + (h ^ a)) * batch + (k ^ b)
                pairs.append((plan.mode_of(h, p, w) * 2 + k, target * 2 + w))
        return pairs

    quarter = plan.size // 4
    parts = [x * quarter for x in (2,2,)]
    now, later = parts[:1], parts[1:]
    jobs = [(0, 0, parts), (1, sum(now), later)]
    first = first_level(plan, leaves, join_order, [(1, 0, now)], VMEM_MOST)
    rest = first_level(plan, leaves, join_order, jobs, VMEM_LIMIT)
    left, right = rest[: len(parts)], first + rest[len(parts) :]
    others = range(1, places)
    messages = []
    arrived = []
    for chunk, blocks in enumerate(parts):
        right_kept, right_sent = right[chunk]
        left_kept, left_sent = left[chunk]
        right_sent = lax.ppermute(right_sent, "mode", over_ways)
        kept_there = [lax.ppermute(right_kept, "mode", over_places(step)) for step in others]
        left_sent = lax.ppermute(left_sent, "mode", over_ways)
        sent_there = [lax.ppermute(right_sent, "mode", over_places(step)) for step in others]
        operands = [
            left_kept,
            left_sent,
            right_kept,
            right_sent,
            *kept_there,
            *sent_there,
            *arrived[1:],
        ]

        def pick(refs):
            there = refs[4 : 2 + 2 * places]
            pairs = list(zip(there[: places - 1], there[places - 1 :]))
            return refs[0], refs[1], refs[2], refs[3], pairs

        rows = second_level(plan, blocks, operands, pick)
        arrived = [
            lax.ppermute(value, ("mode", "branch"), to_rows(a, b))
            for value, (a, b) in zip(rows, plan.steps)
        ]
        messages.append(arrived)
    top_other = top_for_other(plan, join_order, messages)
    top_received = lax.ppermute(top_other, "branch", [(0, 1), (1, 0)])
    amplitudes = own_amplitudes(plan, join_order, slice_values, boundary, messages)
    return other_amplitudes(plan, slice_values, boundary, top_received, amplitudes)


def solution(mesh):
    in_specs = (P("branch", None, ("cuts", "mode"), None, None), P(), P(("cuts", "mode")), P())
    out_specs = P(None, ("cuts", "mode"), "branch", None)
    return jax.shard_map(
        per_device, mesh=mesh, in_specs=in_specs, out_specs=out_specs, check_vma=False
    )
```

```python
import functools

import jax
import jax.numpy as jnp
from jax import lax
from jax.experimental import pallas as pl
from jax.experimental.pallas import tpu as pltpu
from jax.sharding import PartitionSpec as P

ANY = pl.BlockSpec(memory_space=pl.ANY)
SMEM = pl.BlockSpec(memory_space=pltpu.SMEM)
VMEM = pl.BlockSpec(memory_space=pltpu.VMEM)
VMEM_LIMIT = 40 * 2**20
VMEM_MOST = 60 * 2**20


def complex_dot(left_real, left_imag, right):
    left = jnp.concatenate(
        [
            jnp.concatenate([left_real, -left_imag], axis=1),
            jnp.concatenate([left_imag, left_real], axis=1),
        ],
        axis=0,
    )
    sums = jnp.dot(left, right, preferred_element_type=jnp.float32)
    rows = left_real.shape[0]
    return sums[:rows], sums[rows:]


class Copies:
    def __init__(self, sems):
        self.sems = sems
        self.used = 0

    def start(self, source, target):
        copy = pltpu.make_async_copy(source, target, self.sems.at[self.used])
        self.used += 1
        copy.start()
        return copy


def run_kernel(body, outs, scratch, copies, flops, operands, specs, aliases=None, limit=VMEM_LIMIT):
    moved = sum(x.size * x.dtype.itemsize for x in outs) + 2**21
    return pl.pallas_call(
        body,
        out_shape=outs,
        in_specs=specs,
        out_specs=[ANY] * len(outs),
        scratch_shapes=list(scratch) + [pltpu.SemaphoreType.DMA((copies,))],
        input_output_aliases=aliases or {},
        compiler_params=pltpu.CompilerParams(vmem_limit_bytes=limit),
        cost_estimate=pl.CostEstimate(flops=flops, bytes_accessed=moved, transcendentals=0),
    )(*operands)


class Plan:
    def __init__(self, leaves):
        self.modes = lax.axis_size("mode")
        self.batch = leaves.shape[2]
        self.width = leaves.shape[4]
        self.rows = self.width // self.modes
        self.size = self.modes // self.batch
        self.ways = self.batch
        self.places = self.size // self.ways
        assert self.batch == 2 and lax.axis_size("branch") == 2
        self.steps = [(1, 1), (1, 0), (0, 1), (0, 0)]

    def mode_of(self, high, place, way):
        return (high * self.places + place) * self.ways + way

    def here(self):
        mode = lax.axis_index("mode")
        return mode // self.size, (mode % self.size) // self.ways, mode % self.ways


def first_level(plan, leaves, join_order, jobs, limit):
    width, batch, rows, ways = plan.width, plan.batch, plan.rows, plan.ways
    half = width // ways
    chunks = [blocks for _, _, parts in jobs for blocks in parts]
    totals = [sum(parts) * rows for _, _, parts in jobs]

    def body(order, leaf, *rest):
        outs, rest = rest[: 2 * len(chunks)], rest[2 * len(chunks) :]
        copies = Copies(rest[-1])
        branch = lax.axis_index("branch")
        _, _, way = plan.here()
        loads = []
        for index, (role, begin, parts) in enumerate(jobs):
            upper, lower, _ = rest[3 * index : 3 * index + 3]
            pair = jnp.where(order[2 * lax.axis_size("branch") + branch] == 1, 1 - role, role)
            swapped = jnp.where(order[2 * branch + pair] == 1, 1, 0)
            first, second = 2 * pair + swapped, 2 * pair + 1 - swapped
            for item in range(batch):
                mine = [copies.start(leaf.at[second, :, item], lower.at[item])]
                for side, target in enumerate((way, 1 - way)):
                    span = pl.ds(target * half + begin * rows, totals[index])
                    source = leaf.at[first, :, item, span]
                    mine.append(copies.start(source, upper.at[item, :, side]))
                loads.append(mine)
        stores = []
        given = 0
        for index, (role, begin, parts) in enumerate(jobs):
            upper, lower, result = rest[3 * index : 3 * index + 3]
            total = totals[index]
            for item in range(batch):
                for copy in loads[index * batch + item]:
                    copy.wait()
                sums = complex_dot(
                    upper[item, 0].reshape(ways * total, width),
                    upper[item, 1].reshape(ways * total, width),
                    lower[item].reshape(2 * width, width),
                )
                for part in range(2):
                    result[item, part] = (
                        sums[part].astype(jnp.bfloat16).reshape(ways, total // rows, rows, width)
                    )
                for side in range(ways):
                    done = 0
                    for chunk, blocks in enumerate(parts):
                        source = result.at[item, :, side, pl.ds(done, blocks)]
                        place = outs[2 * (given + chunk) + side].at[:, :, item]
                        stores.append(copies.start(source, place))
                        done += blocks
            given += len(parts)
        for copy in stores:
            copy.wait()

    outs = [
        jax.ShapeDtypeStruct((2, blocks, batch, rows, width), jnp.bfloat16)
        for blocks in chunks
        for _ in range(ways)
    ]
    scratch = []
    for total in totals:
        scratch += [
            pltpu.VMEM((batch, 2, ways, total, width), jnp.bfloat16),
            pltpu.VMEM((batch, 2, width, width), jnp.bfloat16),
            pltpu.VMEM((batch, 2, ways, total // rows, rows, width), jnp.bfloat16),
        ]
    copies = len(jobs) * batch * (1 + ways) + batch * ways * len(chunks)
    flops = 8 * batch * ways * sum(totals) * width**2
    results = run_kernel(
        body, outs, scratch, copies, flops, [join_order, leaves], [SMEM, ANY], limit=limit
    )
    return [results[2 * index : 2 * index + 2] for index in range(len(chunks))]


def second_level(plan, blocks, operands, pick):
    width, batch, rows, ways, places = plan.width, plan.batch, plan.rows, plan.ways, plan.places
    held = ways * batch * rows

    def body(*refs):
        left_kept, left_sent, right_kept, right_sent, others = pick(refs[: len(operands)])
        rest = refs[len(operands) :]
        outs, (left, right, result, sems) = rest[:-4], rest[-4:]
        copies = Copies(sems)
        branch = lax.axis_index("branch")
        high, place, way = plan.here()
        loads = []
        for block in range(blocks):
            mine = [
                copies.start(right_kept.at[:, block], right.at[:, block, place, way]),
                copies.start(right_sent.at[:, block], right.at[:, block, place, 1 - way]),
            ]
            for step, (kept, sent) in enumerate(others):
                other = place ^ (step + 1)
                mine.append(copies.start(kept.at[:, block], right.at[:, block, other, way]))
                mine.append(copies.start(sent.at[:, block], right.at[:, block, other, 1 - way]))
            mine.append(copies.start(left_kept.at[:, block], left.at[:, block, way]))
            mine.append(copies.start(left_sent.at[:, block], left.at[:, block, 1 - way]))
            loads.append(mine)
        stores = []
        for block in range(blocks):
            for copy in loads[block]:
                copy.wait()
            halves = [
                jnp.concatenate([left[part, block, high ^ a, branch ^ b] for a, b in plan.steps], axis=0)
                for part in range(2)
            ]
            parts = complex_dot(
                halves[0],
                halves[1],
                jnp.concatenate(
                    [right[part, block].reshape(width, width) for part in range(2)], axis=0
                ),
            )
            for part in range(2):
                result[block, part] = (
                    parts[part].astype(jnp.bfloat16).reshape(ways * batch, rows, width)
                )
            for index in range(ways * batch):
                stores.append(copies.start(result.at[block, :, index], outs[index].at[:, block]))
        for copy in stores:
            copy.wait()

    outs = [jax.ShapeDtypeStruct((2, blocks, rows, width), jnp.bfloat16)] * (ways * batch)
    scratch = [
        pltpu.VMEM((2, blocks, ways, batch, rows, width), jnp.bfloat16),
        pltpu.VMEM((2, blocks, places, ways, batch, rows, width), jnp.bfloat16),
        pltpu.VMEM((blocks, 2, ways * batch, rows, width), jnp.bfloat16),
    ]
    copies = blocks * (2 + 2 * places + ways * batch)
    flops = 8 * blocks * held * width * width
    return run_kernel(body, outs, scratch, copies, flops, operands, [ANY] * len(operands))


def load_operands(plan, copies, order, messages, chunk_blocks, scratch):
    mode = lax.axis_index("mode")
    near, item = (mode // plan.batch) % plan.ways, mode % plan.batch
    top = jnp.where(order[order.shape[0] - 1] == 1, 1, 0)
    loads = []
    begin = 0
    for chunk, blocks in zip(messages, chunk_blocks):
        for (a, b), message in zip(plan.steps, chunk):
            role = item ^ b ^ top
            loads.append(
                copies.start(message, scratch.at[role, :, pl.ds(begin, blocks), near ^ a])
            )
        begin += blocks
    return loads


def top_operands(plan, scratch, half):
    width = plan.width
    kept = plan.size // 2
    left = [
        scratch[0, part, pl.ds(half * kept, kept)].reshape(width // 2, width) for part in range(2)
    ]
    right = jnp.concatenate([scratch[1, part].reshape(width, width) for part in range(2)], axis=0)
    return left[0], left[1], right


def top_scratch(plan):
    return pltpu.VMEM((2, 2, plan.size, plan.batch, plan.rows, plan.width), jnp.bfloat16)


def top_half(plan, join_order, messages, own):
    flat = [message for chunk in messages for message in chunk]
    count = len(messages[0])
    chunk_blocks = [chunk[0].shape[1] for chunk in messages]
    half_shape = (2, plan.width // 2, plan.width)

    def body(order, *refs):
        sources, (out, operands, result, sems) = refs[: len(flat)], refs[len(flat) :]
        copies = Copies(sems)
        core = lax.axis_index("branch")
        grouped = [sources[i : i + count] for i in range(0, len(flat), count)]
        for copy in load_operands(plan, copies, order, grouped, chunk_blocks, operands):
            copy.wait()
        parts = complex_dot(*top_operands(plan, operands, core if own else 1 - core))
        for part in range(2):
            result[part] = parts[part].astype(jnp.bfloat16)
        copies.start(result, out).wait()

    return run_kernel(
        body,
        [jax.ShapeDtypeStruct(half_shape, jnp.bfloat16)],
        [top_scratch(plan), pltpu.VMEM(half_shape, jnp.bfloat16)],
        len(flat) + 1,
        4 * plan.width**3,
        [join_order, *flat],
        [SMEM] + [ANY] * len(flat),
    )[0]


def boundary_products(plan, slice_values, boundary, top_own, top_received):
    width = plan.width
    shape = (2, plan.batch, width // 2, width)

    def body(values, bound, own, received, out, result, sems):
        copies = Copies(sems)
        core = lax.axis_index("branch")
        stores = []
        for index, (top, item) in enumerate(((own, core), (received, 1 - core))):
            value = jnp.where(values[item] == 1, 1, 0)
            chosen = bound[value].reshape(2 * width, width)
            parts = complex_dot(top[0], top[1], chosen)
            for part in range(2):
                result[index, part] = parts[part]
            stores.append(copies.start(result.at[index], out.at[:, item]))
        for copy in stores:
            copy.wait()

    return run_kernel(
        body,
        [jax.ShapeDtypeStruct(shape, jnp.float32)],
        [pltpu.VMEM((plan.batch, 2, width // 2, width), jnp.float32)],
        plan.batch,
        8 * width**3,
        [slice_values, boundary, top_own, top_received],
        [SMEM, VMEM, VMEM, VMEM],
    )[0]


def per_device(leaves, join_order, slice_values, boundary):
    plan = Plan(leaves)
    modes, ways, places, batch = plan.modes, plan.ways, plan.places, plan.batch
    every = [
        (high, place, way)
        for high in range(batch)
        for place in range(places)
        for way in range(ways)
    ]
    over_ways = [(plan.mode_of(h, p, w), plan.mode_of(h, p, w ^ 1)) for h, p, w in every]

    def over_places(step):
        return [(plan.mode_of(h, p, w), plan.mode_of(h, p ^ step, w)) for h, p, w in every]

    def to_rows(a, b):
        pairs = []
        for h, p, w in every:
            for k in range(2):
                target = (p * ways + (h ^ a)) * batch + (k ^ b)
                pairs.append((plan.mode_of(h, p, w) * 2 + k, target * 2 + w))
        return pairs

    quarter = plan.size // 4
    parts = [x * quarter for x in (2, 2)]
    now, later = parts[:1], parts[1:]
    jobs = [(0, 0, parts), (1, sum(now), later)]
    first = first_level(plan, leaves, join_order, [(1, 0, now)], VMEM_MOST)
    rest = first_level(plan, leaves, join_order, jobs, VMEM_LIMIT)
    left, right = rest[: len(parts)], first + rest[len(parts) :]
    others = range(1, places)
    messages = []
    arrived = []
    for chunk, blocks in enumerate(parts):
        right_kept, right_sent = right[chunk]
        left_kept, left_sent = left[chunk]
        right_sent = lax.ppermute(right_sent, "mode", over_ways)
        kept_there = [lax.ppermute(right_kept, "mode", over_places(step)) for step in others]
        left_sent = lax.ppermute(left_sent, "mode", over_ways)
        sent_there = [lax.ppermute(right_sent, "mode", over_places(step)) for step in others]
        operands = [
            left_kept,
            left_sent,
            right_kept,
            right_sent,
            *kept_there,
            *sent_there,
            *arrived[2:],
        ]

        def pick(refs):
            there = refs[4 : 2 + 2 * places]
            pairs = list(zip(there[: places - 1], there[places - 1 :]))
            return refs[0], refs[1], refs[2], refs[3], pairs

        rows = second_level(plan, blocks, operands, pick)
        arrived = [
            lax.ppermute(value, ("mode", "branch"), to_rows(a, b))
            for value, (a, b) in zip(rows, plan.steps)
        ]
        messages.append(arrived)
    top_other = top_half(plan, join_order, messages, False)
    top_received = lax.ppermute(top_other, "branch", [(0, 1), (1, 0)])
    top_own = top_half(plan, join_order, messages, True)
    return boundary_products(plan, slice_values, boundary, top_own, top_received)


def solution(mesh):
    in_specs = (P("branch", None, ("cuts", "mode"), None, None), P(), P(("cuts", "mode")), P())
    out_specs = P(None, ("cuts", "mode"), "branch", None)
    return jax.shard_map(
        per_device, mesh=mesh, in_specs=in_specs, out_specs=out_specs, check_vma=False
    )
```

```python
import functools

import jax
import jax.numpy as jnp
from jax import lax
from jax.experimental import pallas as pl
from jax.experimental.pallas import tpu as pltpu
from jax.sharding import PartitionSpec as P

ANY = pl.BlockSpec(memory_space=pl.ANY)
SMEM = pl.BlockSpec(memory_space=pltpu.SMEM)
VMEM = pl.BlockSpec(memory_space=pltpu.VMEM)
VMEM_LIMIT = 40 * 2**20
VMEM_MOST = 60 * 2**20


def complex_dot(left_real, left_imag, right):
    left = jnp.concatenate(
        [
            jnp.concatenate([left_real, -left_imag], axis=1),
            jnp.concatenate([left_imag, left_real], axis=1),
        ],
        axis=0,
    )
    sums = jnp.dot(left, right, preferred_element_type=jnp.float32)
    rows = left_real.shape[0]
    return sums[:rows], sums[rows:]


class Copies:
    def __init__(self, sems):
        self.sems = sems
        self.used = 0

    def start(self, source, target):
        copy = pltpu.make_async_copy(source, target, self.sems.at[self.used])
        self.used += 1
        copy.start()
        return copy


def run_kernel(
    body, outs, scratch, copies, flops, operands, specs, limit=VMEM_LIMIT, place=ANY
):
    moved = sum(x.size * x.dtype.itemsize for x in outs) + 2**21
    return pl.pallas_call(
        body,
        out_shape=outs,
        in_specs=specs,
        out_specs=[place] * len(outs),
        scratch_shapes=list(scratch) + [pltpu.SemaphoreType.DMA((copies,))],
        compiler_params=pltpu.CompilerParams(vmem_limit_bytes=limit),
        cost_estimate=pl.CostEstimate(flops=flops, bytes_accessed=moved, transcendentals=0),
    )(*operands)


class Plan:
    def __init__(self, leaves):
        self.modes = lax.axis_size("mode")
        self.batch = leaves.shape[2]
        self.width = leaves.shape[4]
        self.rows = self.width // self.modes
        self.size = self.modes // self.batch
        self.ways = self.batch
        self.places = self.size // self.ways
        assert self.batch == 2 and lax.axis_size("branch") == 2
        self.steps = [(1, 1), (1, 0), (0, 1), (0, 0)]

    def mode_of(self, high, place, way):
        return (high * self.places + place) * self.ways + way

    def here(self):
        mode = lax.axis_index("mode")
        return mode // self.size, (mode % self.size) // self.ways, mode % self.ways


def first_level(plan, leaves, join_order, jobs, limit):
    width, batch, rows, ways = plan.width, plan.batch, plan.rows, plan.ways
    half = width // ways
    chunks = [blocks for _, _, parts in jobs for blocks in parts]
    totals = [sum(parts) * rows for _, _, parts in jobs]

    def body(order, leaf, *rest):
        outs, rest = rest[: 2 * len(chunks)], rest[2 * len(chunks) :]
        copies = Copies(rest[-1])
        branch = lax.axis_index("branch")
        _, _, way = plan.here()
        loads = []
        for index, (role, begin, parts) in enumerate(jobs):
            upper, lower, _ = rest[3 * index : 3 * index + 3]
            pair = jnp.where(order[2 * lax.axis_size("branch") + branch] == 1, 1 - role, role)
            swapped = jnp.where(order[2 * branch + pair] == 1, 1, 0)
            first, second = 2 * pair + swapped, 2 * pair + 1 - swapped
            for item in range(batch):
                mine = [copies.start(leaf.at[second, :, item], lower.at[item])]
                for side, target in enumerate((way, 1 - way)):
                    span = pl.ds(target * half + begin * rows, totals[index])
                    source = leaf.at[first, :, item, span]
                    mine.append(copies.start(source, upper.at[item, :, side]))
                loads.append(mine)
        stores = []
        given = 0
        for index, (role, begin, parts) in enumerate(jobs):
            upper, lower, result = rest[3 * index : 3 * index + 3]
            total = totals[index]
            for item in range(batch):
                for copy in loads[index * batch + item]:
                    copy.wait()
                sums = complex_dot(
                    upper[item, 0].reshape(ways * total, width),
                    upper[item, 1].reshape(ways * total, width),
                    lower[item].reshape(2 * width, width),
                )
                for part in range(2):
                    result[item, part] = (
                        sums[part].astype(jnp.bfloat16).reshape(ways, total // rows, rows, width)
                    )
                for side in range(ways):
                    done = 0
                    for chunk, blocks in enumerate(parts):
                        source = result.at[item, :, side, pl.ds(done, blocks)]
                        place = outs[2 * (given + chunk) + side].at[:, :, item]
                        stores.append(copies.start(source, place))
                        done += blocks
            given += len(parts)
        for copy in stores:
            copy.wait()

    outs = [
        jax.ShapeDtypeStruct((2, blocks, batch, rows, width), jnp.bfloat16)
        for blocks in chunks
        for _ in range(ways)
    ]
    scratch = []
    for total in totals:
        scratch += [
            pltpu.VMEM((batch, 2, ways, total, width), jnp.bfloat16),
            pltpu.VMEM((batch, 2, width, width), jnp.bfloat16),
            pltpu.VMEM((batch, 2, ways, total // rows, rows, width), jnp.bfloat16),
        ]
    copies = len(jobs) * batch * (1 + ways) + batch * ways * len(chunks)
    flops = 8 * batch * ways * sum(totals) * width**2
    results = run_kernel(
        body, outs, scratch, copies, flops, [join_order, leaves], [SMEM, ANY], limit=limit
    )
    return [results[2 * index : 2 * index + 2] for index in range(len(chunks))]


def once_there(value, after):
    def body(*refs):
        pass

    return pl.pallas_call(
        body,
        out_shape=jax.ShapeDtypeStruct(value.shape, value.dtype),
        in_specs=[ANY] * (1 + len(after)),
        out_specs=ANY,
        input_output_aliases={0: 0},
        compiler_params=pltpu.CompilerParams(vmem_limit_bytes=2**20),
    )(value, *after)


def arrival(after, micros):
    def body(*refs):
        refs[-1][...] = jnp.zeros((8, 128), jnp.float32)

    return pl.pallas_call(
        body,
        out_shape=jax.ShapeDtypeStruct((8, 128), jnp.float32),
        in_specs=[ANY] * len(after),
        out_specs=VMEM,
        compiler_params=pltpu.CompilerParams(vmem_limit_bytes=2**20),
        cost_estimate=pl.CostEstimate(
            flops=micros * 10**9, bytes_accessed=micros * 3 * 10**6, transcendentals=0
        ),
    )(*after)


def second_level(plan, blocks, operands, pick):
    width, batch, rows, ways, places = plan.width, plan.batch, plan.rows, plan.ways, plan.places
    held = ways * batch * rows

    def body(*refs):
        left_kept, left_sent, right_kept, right_sent, others = pick(refs[: len(operands)])
        rest = refs[len(operands) :]
        outs, (left, right, result, sems) = rest[:-4], rest[-4:]
        copies = Copies(sems)
        branch = lax.axis_index("branch")
        high, place, way = plan.here()
        loads = []
        for block in range(blocks):
            mine = [
                copies.start(right_kept(block), right.at[:, block, place, way]),
                copies.start(right_sent(block), right.at[:, block, place, 1 - way]),
            ]
            for step, (kept, sent) in enumerate(others):
                other = place ^ (step + 1)
                mine.append(copies.start(kept(block), right.at[:, block, other, way]))
                mine.append(copies.start(sent(block), right.at[:, block, other, 1 - way]))
            mine.append(copies.start(left_kept(block), left.at[:, block, way]))
            mine.append(copies.start(left_sent(block), left.at[:, block, 1 - way]))
            loads.append(mine)
        stores = []
        for block in range(blocks):
            for copy in loads[block]:
                copy.wait()
            halves = [
                jnp.concatenate([left[part, block, high ^ a, branch ^ b] for a, b in plan.steps], axis=0)
                for part in range(2)
            ]
            parts = complex_dot(
                halves[0],
                halves[1],
                jnp.concatenate(
                    [right[part, block].reshape(width, width) for part in range(2)], axis=0
                ),
            )
            for part in range(2):
                result[block, part] = (
                    parts[part].astype(jnp.bfloat16).reshape(ways * batch, rows, width)
                )
            for index in range(ways * batch):
                stores.append(copies.start(result.at[block, :, index], outs[index].at[:, block]))
        for copy in stores:
            copy.wait()

    outs = [jax.ShapeDtypeStruct((2, blocks, rows, width), jnp.bfloat16)] * (ways * batch)
    scratch = [
        pltpu.VMEM((2, blocks, ways, batch, rows, width), jnp.bfloat16),
        pltpu.VMEM((2, blocks, places, ways, batch, rows, width), jnp.bfloat16),
        pltpu.VMEM((blocks, 2, ways * batch, rows, width), jnp.bfloat16),
    ]
    copies = blocks * (2 + 2 * places + ways * batch)
    flops = 8 * blocks * held * width * width
    return run_kernel(body, outs, scratch, copies, flops, operands, [ANY] * len(operands))


def place_operands(plan, order, messages, chunk_blocks, scratch):
    mode = lax.axis_index("mode")
    near, item = (mode // plan.batch) % plan.ways, mode % plan.batch
    top = jnp.where(order[order.shape[0] - 1] == 1, 1, 0)
    begin = 0
    for chunk, blocks in zip(messages, chunk_blocks):
        for (a, b), message in zip(plan.steps, chunk):
            scratch[item ^ b ^ top, :, pl.ds(begin, blocks), near ^ a] = message[...]
        begin += blocks


def top_operands(plan, scratch, half):
    width = plan.width
    kept = plan.size // 2
    left = [
        scratch[0, part, pl.ds(half * kept, kept)].reshape(width // 2, width) for part in range(2)
    ]
    right = jnp.concatenate([scratch[1, part].reshape(width, width) for part in range(2)], axis=0)
    return left[0], left[1], right


def top_scratch(plan):
    return pltpu.VMEM((2, 2, plan.size, plan.batch, plan.rows, plan.width), jnp.bfloat16)


def top_half(plan, join_order, messages, own):
    flat = [message for chunk in messages for message in chunk]
    count = len(messages[0])
    chunk_blocks = [chunk[0].shape[1] for chunk in messages]
    half_shape = (2, plan.width // 2, plan.width)

    def body(order, *refs):
        sources, (out, operands, _) = refs[: len(flat)], refs[len(flat) :]
        core = lax.axis_index("branch")
        grouped = [sources[i : i + count] for i in range(0, len(flat), count)]
        place_operands(plan, order, grouped, chunk_blocks, operands)
        parts = complex_dot(*top_operands(plan, operands, core if own else 1 - core))
        for part in range(2):
            out[part] = parts[part].astype(jnp.bfloat16)

    return run_kernel(
        body,
        [jax.ShapeDtypeStruct(half_shape, jnp.bfloat16)],
        [top_scratch(plan)],
        1,
        4 * plan.width**3,
        [join_order, *flat],
        [SMEM] + [VMEM] * len(flat),
        place=VMEM,
    )[0]


def boundary_products(plan, slice_values, boundary, top_own, top_received):
    width = plan.width
    shape = (2, plan.batch, width // 2, width)

    def body(values, bound, own, received, out, result, sems):
        copies = Copies(sems)
        core = lax.axis_index("branch")
        stores = []
        for index, (top, item) in enumerate(((own, core), (received, 1 - core))):
            value = jnp.where(values[item] == 1, 1, 0)
            chosen = bound[value].reshape(2 * width, width)
            parts = complex_dot(top[0], top[1], chosen)
            for part in range(2):
                result[index, part] = parts[part]
            stores.append(copies.start(result.at[index], out.at[:, item]))
        for copy in stores:
            copy.wait()

    return run_kernel(
        body,
        [jax.ShapeDtypeStruct(shape, jnp.float32)],
        [pltpu.VMEM((plan.batch, 2, width // 2, width), jnp.float32)],
        plan.batch,
        8 * width**3,
        [slice_values, boundary, top_own, top_received],
        [SMEM, VMEM, VMEM, VMEM],
    )[0]


def per_device(leaves, join_order, slice_values, boundary):
    plan = Plan(leaves)
    modes, ways, places, batch = plan.modes, plan.ways, plan.places, plan.batch
    every = [
        (high, place, way)
        for high in range(batch)
        for place in range(places)
        for way in range(ways)
    ]
    over_ways = [(plan.mode_of(h, p, w), plan.mode_of(h, p, w ^ 1)) for h, p, w in every]

    def over_places(step):
        return [(plan.mode_of(h, p, w), plan.mode_of(h, p ^ step, w)) for h, p, w in every]

    def to_rows(a, b):
        pairs = []
        for h, p, w in every:
            for k in range(2):
                target = (p * ways + (h ^ a)) * batch + (k ^ b)
                pairs.append((plan.mode_of(h, p, w) * 2 + k, target * 2 + w))
        return pairs

    quarter = plan.size // 4
    parts = [2 * quarter, 2 * quarter]
    pieces = [[2 * quarter], [quarter, quarter]]
    right = first_level(plan, leaves, join_order, [(1, 0, parts[:1])], VMEM_MOST)
    rest = first_level(plan, leaves, join_order, [(0, 0, parts), (1, parts[0], parts[1:])], VMEM_LIMIT)
    left, right = rest[: len(parts)], right + rest[len(parts) :]
    others = range(1, places)
    messages = []
    for chunk in range(len(parts)):
        left_kept, left_send = left[chunk]
        right_kept, right_send = right[chunk]
        right_sent = lax.ppermute(right_send, "mode", over_ways)
        kept_there = [lax.ppermute(right_kept, "mode", over_places(step)) for step in others]
        left_sent = lax.ppermute(left_send, "mode", over_ways)
        lows = [sum(pieces[chunk][:piece]) for piece in range(len(pieces[chunk]))]
        forward = [right_sent]
        if chunk:
            forward = [
                right_sent[:, low : low + count] for low, count in zip(lows, pieces[chunk])
            ]
            forward[1:] = [once_there(value, [messages[-1][0]]) for value in forward[1:]]
        sent_there = [
            [lax.ppermute(value, "mode", over_places(step)) for step in others]
            for value in forward
        ]
        for piece, (low, count) in enumerate(zip(lows, pieces[chunk])):
            extra = []
            if chunk and piece == 0:
                extra = [messages[-1][2], arrival([*messages[-1][:2], kept_there[0]], 5)]
            elif piece:
                extra = [messages[-2][3]]
            operands = [left_kept, left_sent, right_kept, right_sent]
            operands += [*kept_there, *sent_there[piece], *extra]

            def pick(refs, low=low):
                def by(ref, base):
                    return lambda block: ref.at[:, base + block]

                there = refs[4 : 2 + 2 * places]
                kept, sent = there[: places - 1], there[places - 1 :]
                pairs = [(by(one, low), by(two, 0)) for one, two in zip(kept, sent)]
                return *[by(ref, low) for ref in refs[:4]], pairs

            rows = second_level(plan, count, operands, pick)
            messages.append(
                [
                    lax.ppermute(value, ("mode", "branch"), to_rows(a, b))
                    for value, (a, b) in zip(rows, plan.steps)
                ]
            )
    top_other = top_half(plan, join_order, messages, False)
    top_received = lax.ppermute(top_other, "branch", [(0, 1), (1, 0)])
    top_own = top_half(plan, join_order, messages, True)
    return boundary_products(plan, slice_values, boundary, top_own, top_received)


def solution(mesh):
    in_specs = (P("branch", None, ("cuts", "mode"), None, None), P(), P(("cuts", "mode")), P())
    out_specs = P(None, ("cuts", "mode"), "branch", None)
    return jax.shard_map(
        per_device, mesh=mesh, in_specs=in_specs, out_specs=out_specs, check_vma=False
    )
```

```python
import functools

import jax
import jax.numpy as jnp
from jax import lax
from jax.experimental import pallas as pl
from jax.experimental.pallas import tpu as pltpu
from jax.sharding import PartitionSpec as P

ANY = pl.BlockSpec(memory_space=pl.ANY)
SMEM = pl.BlockSpec(memory_space=pltpu.SMEM)
VMEM = pl.BlockSpec(memory_space=pltpu.VMEM)
VMEM_LIMIT = 40 * 2**20
VMEM_MOST = 60 * 2**20


def complex_dot(left_real, left_imag, right):
    left = jnp.concatenate(
        [
            jnp.concatenate([left_real, -left_imag], axis=1),
            jnp.concatenate([left_imag, left_real], axis=1),
        ],
        axis=0,
    )
    sums = jnp.dot(left, right, preferred_element_type=jnp.float32)
    rows = left_real.shape[0]
    return sums[:rows], sums[rows:]


class Copies:
    def __init__(self, sems):
        self.sems = sems
        self.used = 0

    def start(self, source, target):
        copy = pltpu.make_async_copy(source, target, self.sems.at[self.used])
        self.used += 1
        copy.start()
        return copy


def run_kernel(
    body, outs, scratch, copies, flops, operands, specs, limit=VMEM_LIMIT, place=ANY
):
    moved = sum(x.size * x.dtype.itemsize for x in outs) + 2**21
    return pl.pallas_call(
        body,
        out_shape=outs,
        in_specs=specs,
        out_specs=[place] * len(outs),
        scratch_shapes=list(scratch) + [pltpu.SemaphoreType.DMA((copies,))],
        compiler_params=pltpu.CompilerParams(vmem_limit_bytes=limit),
        cost_estimate=pl.CostEstimate(flops=flops, bytes_accessed=moved, transcendentals=0),
    )(*operands)


class Plan:
    def __init__(self, leaves):
        self.modes = lax.axis_size("mode")
        self.batch = leaves.shape[2]
        self.width = leaves.shape[4]
        self.rows = self.width // self.modes
        self.size = self.modes // self.batch
        self.ways = self.batch
        self.places = self.size // self.ways
        assert self.batch == 2 and lax.axis_size("branch") == 2
        self.steps = [(1, 1), (1, 0), (0, 1), (0, 0)]

    def mode_of(self, high, place, way):
        return (high * self.places + place) * self.ways + way

    def here(self):
        mode = lax.axis_index("mode")
        return mode // self.size, (mode % self.size) // self.ways, mode % self.ways


def first_level(plan, leaves, join_order, jobs, limit):
    width, batch, rows, ways = plan.width, plan.batch, plan.rows, plan.ways
    half = width // ways
    chunks = [blocks for _, _, parts in jobs for blocks in parts]
    totals = [sum(parts) * rows for _, _, parts in jobs]

    def body(order, leaf, *rest):
        outs, rest = rest[: 2 * len(chunks)], rest[2 * len(chunks) :]
        copies = Copies(rest[-1])
        branch = lax.axis_index("branch")
        _, _, way = plan.here()
        loads = []
        for index, (role, begin, parts) in enumerate(jobs):
            upper, lower, _ = rest[3 * index : 3 * index + 3]
            pair = jnp.where(order[2 * lax.axis_size("branch") + branch] == 1, 1 - role, role)
            swapped = jnp.where(order[2 * branch + pair] == 1, 1, 0)
            first, second = 2 * pair + swapped, 2 * pair + 1 - swapped
            for item in range(batch):
                mine = [copies.start(leaf.at[second, :, item], lower.at[item])]
                for side, target in enumerate((way, 1 - way)):
                    span = pl.ds(target * half + begin * rows, totals[index])
                    source = leaf.at[first, :, item, span]
                    mine.append(copies.start(source, upper.at[item, :, side]))
                loads.append(mine)
        stores = []
        given = 0
        for index, (role, begin, parts) in enumerate(jobs):
            upper, lower, result = rest[3 * index : 3 * index + 3]
            total = totals[index]
            for item in range(batch):
                for copy in loads[index * batch + item]:
                    copy.wait()
                sums = complex_dot(
                    upper[item, 0].reshape(ways * total, width),
                    upper[item, 1].reshape(ways * total, width),
                    lower[item].reshape(2 * width, width),
                )
                for part in range(2):
                    result[item, part] = (
                        sums[part].astype(jnp.bfloat16).reshape(ways, total // rows, rows, width)
                    )
                for side in range(ways):
                    done = 0
                    for chunk, blocks in enumerate(parts):
                        source = result.at[item, :, side, pl.ds(done, blocks)]
                        place = outs[2 * (given + chunk) + side].at[:, :, item]
                        stores.append(copies.start(source, place))
                        done += blocks
            given += len(parts)
        for copy in stores:
            copy.wait()

    outs = [
        jax.ShapeDtypeStruct((2, blocks, batch, rows, width), jnp.bfloat16)
        for blocks in chunks
        for _ in range(ways)
    ]
    scratch = []
    for total in totals:
        scratch += [
            pltpu.VMEM((batch, 2, ways, total, width), jnp.bfloat16),
            pltpu.VMEM((batch, 2, width, width), jnp.bfloat16),
            pltpu.VMEM((batch, 2, ways, total // rows, rows, width), jnp.bfloat16),
        ]
    copies = len(jobs) * batch * (1 + ways) + batch * ways * len(chunks)
    flops = 8 * batch * ways * sum(totals) * width**2
    results = run_kernel(
        body, outs, scratch, copies, flops, [join_order, leaves], [SMEM, ANY], limit=limit
    )
    return [results[2 * index : 2 * index + 2] for index in range(len(chunks))]


def once_there(value, after):
    def body(*refs):
        pass

    return pl.pallas_call(
        body,
        out_shape=jax.ShapeDtypeStruct(value.shape, value.dtype),
        in_specs=[ANY] * (1 + len(after)),
        out_specs=ANY,
        input_output_aliases={0: 0},
        compiler_params=pltpu.CompilerParams(vmem_limit_bytes=2**20),
    )(value, *after)


def arrival(after, micros):
    def body(*refs):
        refs[-1][...] = jnp.zeros((8, 128), jnp.float32)

    return pl.pallas_call(
        body,
        out_shape=jax.ShapeDtypeStruct((8, 128), jnp.float32),
        in_specs=[ANY] * len(after),
        out_specs=VMEM,
        compiler_params=pltpu.CompilerParams(vmem_limit_bytes=2**20),
        cost_estimate=pl.CostEstimate(
            flops=micros * 10**9, bytes_accessed=micros * 3 * 10**6, transcendentals=0
        ),
    )(*after)


def second_level(plan, blocks, operands, pick, direct):
    width, batch, rows, ways, places = plan.width, plan.batch, plan.rows, plan.ways, plan.places
    held = ways * batch * rows

    def body(*refs):
        left_kept, left_sent, right_kept, right_sent, others = pick(refs[: len(operands)])
        rest = refs[len(operands) :]
        outs, (left, right, result, sems) = rest[:-4], rest[-4:]
        copies = Copies(sems)
        branch = lax.axis_index("branch")
        high, place, way = plan.here()
        loads = []
        for block in range(blocks):
            moves = [
                (right_kept(block), right.at[:, block, place, way]),
                (right_sent(block), right.at[:, block, place, 1 - way]),
                (left_kept(block), left.at[:, block, way]),
                (left_sent(block), left.at[:, block, 1 - way]),
            ]
            for step, (kept, sent) in enumerate(others):
                other = place ^ (step + 1)
                moves.append((kept(block), right.at[:, block, other, way]))
                moves.append((sent(block), right.at[:, block, other, 1 - way]))
            if direct:
                for source, target in moves:
                    target[...] = source[...]
            else:
                loads.append([copies.start(source, target) for source, target in moves])
        stores = []
        for block in range(blocks):
            for copy in loads[block] if loads else []:
                copy.wait()
            halves = [
                jnp.concatenate([left[part, block, high ^ a, branch ^ b] for a, b in plan.steps], axis=0)
                for part in range(2)
            ]
            parts = complex_dot(
                halves[0],
                halves[1],
                jnp.concatenate(
                    [right[part, block].reshape(width, width) for part in range(2)], axis=0
                ),
            )
            for part in range(2):
                done = parts[part].astype(jnp.bfloat16).reshape(ways * batch, rows, width)
                if direct:
                    for index in range(ways * batch):
                        outs[index][part, block] = done[index]
                else:
                    result[block, part] = done
            if not direct:
                for index in range(ways * batch):
                    source = result.at[block, :, index]
                    stores.append(copies.start(source, outs[index].at[:, block]))
        for copy in stores:
            copy.wait()

    outs = [jax.ShapeDtypeStruct((2, blocks, rows, width), jnp.bfloat16)] * (ways * batch)
    scratch = [
        pltpu.VMEM((2, blocks, ways, batch, rows, width), jnp.bfloat16),
        pltpu.VMEM((2, blocks, places, ways, batch, rows, width), jnp.bfloat16),
        pltpu.VMEM((blocks, 2, ways * batch, rows, width), jnp.bfloat16),
    ]
    copies = blocks * (2 + 2 * places + ways * batch)
    flops = 8 * blocks * held * width * width
    count = 2 + 2 * places if direct else 0
    specs = [VMEM] * count + [ANY] * (len(operands) - count)
    return run_kernel(
        body, outs, scratch, copies, flops, operands, specs, place=VMEM if direct else ANY
    )


def place_operands(plan, order, messages, chunk_blocks, scratch):
    mode = lax.axis_index("mode")
    near, item = (mode // plan.batch) % plan.ways, mode % plan.batch
    top = jnp.where(order[order.shape[0] - 1] == 1, 1, 0)
    begin = 0
    for chunk, blocks in zip(messages, chunk_blocks):
        for (a, b), message in zip(plan.steps, chunk):
            scratch[item ^ b ^ top, :, pl.ds(begin, blocks), near ^ a] = message[...]
        begin += blocks


def top_operands(plan, scratch, half):
    width = plan.width
    kept = plan.size // 2
    left = [
        scratch[0, part, pl.ds(half * kept, kept)].reshape(width // 2, width) for part in range(2)
    ]
    right = jnp.concatenate([scratch[1, part].reshape(width, width) for part in range(2)], axis=0)
    return left[0], left[1], right


def top_scratch(plan):
    return pltpu.VMEM((2, 2, plan.size, plan.batch, plan.rows, plan.width), jnp.bfloat16)


def top_half(plan, join_order, messages, own):
    flat = [message for chunk in messages for message in chunk]
    count = len(messages[0])
    chunk_blocks = [chunk[0].shape[1] for chunk in messages]
    half_shape = (2, plan.width // 2, plan.width)

    def body(order, *refs):
        sources, (out, operands, _) = refs[: len(flat)], refs[len(flat) :]
        core = lax.axis_index("branch")
        grouped = [sources[i : i + count] for i in range(0, len(flat), count)]
        place_operands(plan, order, grouped, chunk_blocks, operands)
        parts = complex_dot(*top_operands(plan, operands, core if own else 1 - core))
        for part in range(2):
            out[part] = parts[part].astype(jnp.bfloat16)

    return run_kernel(
        body,
        [jax.ShapeDtypeStruct(half_shape, jnp.bfloat16)],
        [top_scratch(plan)],
        1,
        4 * plan.width**3,
        [join_order, *flat],
        [SMEM] + [VMEM] * len(flat),
        place=VMEM,
    )[0]


def boundary_products(plan, slice_values, boundary, top_own, top_received):
    width = plan.width
    shape = (2, plan.batch, width // 2, width)

    def body(values, bound, own, received, out, result, sems):
        copies = Copies(sems)
        core = lax.axis_index("branch")
        stores = []
        half = width // 4
        for index, (top, item) in enumerate(((own, core), (received, 1 - core))):
            value = jnp.where(values[item] == 1, 1, 0)
            chosen = bound[value].reshape(2 * width, width)
            for low in range(0, width // 2, half):
                span = pl.ds(low, half)
                parts = complex_dot(top[0, span], top[1, span], chosen)
                for part in range(2):
                    result[index, part, span] = parts[part]
                stores.append(copies.start(result.at[index, :, span], out.at[:, item, span]))
        for copy in stores:
            copy.wait()

    return run_kernel(
        body,
        [jax.ShapeDtypeStruct(shape, jnp.float32)],
        [pltpu.VMEM((plan.batch, 2, width // 2, width), jnp.float32)],
        2 * plan.batch,
        8 * width**3,
        [slice_values, boundary, top_own, top_received],
        [SMEM, VMEM, VMEM, VMEM],
    )[0]


def per_device(leaves, join_order, slice_values, boundary):
    plan = Plan(leaves)
    modes, ways, places, batch = plan.modes, plan.ways, plan.places, plan.batch
    every = [
        (high, place, way)
        for high in range(batch)
        for place in range(places)
        for way in range(ways)
    ]
    over_ways = [(plan.mode_of(h, p, w), plan.mode_of(h, p, w ^ 1)) for h, p, w in every]

    def over_places(step):
        return [(plan.mode_of(h, p, w), plan.mode_of(h, p ^ step, w)) for h, p, w in every]

    def to_rows(a, b):
        pairs = []
        for h, p, w in every:
            for k in range(2):
                target = (p * ways + (h ^ a)) * batch + (k ^ b)
                pairs.append((plan.mode_of(h, p, w) * 2 + k, target * 2 + w))
        return pairs

    quarter = plan.size // 4
    parts = [2 * quarter, 2 * quarter]
    pieces = [[2 * quarter], [quarter, quarter]]
    right = first_level(plan, leaves, join_order, [(1, 0, parts[:1])], VMEM_MOST)
    rest = first_level(plan, leaves, join_order, [(0, 0, parts), (1, parts[0], parts[1:])], VMEM_LIMIT)
    left, right = rest[: len(parts)], right + rest[len(parts) :]
    others = range(1, places)
    messages = []
    for chunk in range(len(parts)):
        left_kept, left_send = left[chunk]
        right_kept, right_send = right[chunk]
        right_sent = lax.ppermute(right_send, "mode", over_ways)
        kept_there = [lax.ppermute(right_kept, "mode", over_places(step)) for step in others]
        left_sent = lax.ppermute(left_send, "mode", over_ways)
        lows = [sum(pieces[chunk][:piece]) for piece in range(len(pieces[chunk]))]
        forward = [right_sent]
        if chunk:
            forward = [
                right_sent[:, low : low + count] for low, count in zip(lows, pieces[chunk])
            ]
            forward[1:] = [once_there(value, [messages[-1][0]]) for value in forward[1:]]
        sent_there = [
            [lax.ppermute(value, "mode", over_places(step)) for step in others]
            for value in forward
        ]
        for piece, (low, count) in enumerate(zip(lows, pieces[chunk])):
            extra = []
            if chunk and piece == 0:
                extra = [messages[-1][2], arrival([*messages[-1][:2], kept_there[0]], 5)]
            elif piece:
                extra = [messages[-2][3]]
            operands = [left_kept, left_sent, right_kept, right_sent]
            operands += [*kept_there, *sent_there[piece], *extra]

            def pick(refs, low=low):
                def by(ref, base):
                    return lambda block: ref.at[:, base + block]

                there = refs[4 : 2 + 2 * places]
                kept, sent = there[: places - 1], there[places - 1 :]
                pairs = [(by(one, low), by(two, 0)) for one, two in zip(kept, sent)]
                return *[by(ref, low) for ref in refs[:4]], pairs

            rows = second_level(plan, count, operands, pick, chunk > 0)
            messages.append(
                [
                    lax.ppermute(value, ("mode", "branch"), to_rows(a, b))
                    for value, (a, b) in zip(rows, plan.steps)
                ]
            )
    top_other = top_half(plan, join_order, messages, False)
    top_received = lax.ppermute(top_other, "branch", [(0, 1), (1, 0)])
    top_own = top_half(plan, join_order, messages, True)
    return boundary_products(plan, slice_values, boundary, top_own, top_received)


def solution(mesh):
    in_specs = (P("branch", None, ("cuts", "mode"), None, None), P(), P(("cuts", "mode")), P())
    out_specs = P(None, ("cuts", "mode"), "branch", None)
    return jax.shard_map(
        per_device, mesh=mesh, in_specs=in_specs, out_specs=out_specs, check_vma=False
    )
```

```python
import functools

import jax
import jax.numpy as jnp
from jax import lax
from jax.experimental import pallas as pl
from jax.experimental.pallas import tpu as pltpu
from jax.sharding import PartitionSpec as P

ANY = pl.BlockSpec(memory_space=pl.ANY)
SMEM = pl.BlockSpec(memory_space=pltpu.SMEM)
VMEM = pl.BlockSpec(memory_space=pltpu.VMEM)
VMEM_LIMIT = 40 * 2**20
VMEM_MOST = 60 * 2**20


def complex_dot(left_real, left_imag, right):
    left = jnp.concatenate(
        [
            jnp.concatenate([left_real, -left_imag], axis=1),
            jnp.concatenate([left_imag, left_real], axis=1),
        ],
        axis=0,
    )
    sums = jnp.dot(left, right, preferred_element_type=jnp.float32)
    rows = left_real.shape[0]
    return sums[:rows], sums[rows:]


class Copies:
    def __init__(self, sems):
        self.sems = sems
        self.used = 0

    def start(self, source, target):
        copy = pltpu.make_async_copy(source, target, self.sems.at[self.used])
        self.used += 1
        copy.start()
        return copy


def run_kernel(
    body, outs, scratch, copies, flops, operands, specs, limit=VMEM_LIMIT, place=ANY
):
    moved = sum(x.size * x.dtype.itemsize for x in outs) + 2**21
    return pl.pallas_call(
        body,
        out_shape=outs,
        in_specs=specs,
        out_specs=[place] * len(outs),
        scratch_shapes=list(scratch) + [pltpu.SemaphoreType.DMA((copies,))],
        compiler_params=pltpu.CompilerParams(vmem_limit_bytes=limit),
        cost_estimate=pl.CostEstimate(flops=flops, bytes_accessed=moved, transcendentals=0),
    )(*operands)


class Plan:
    def __init__(self, leaves):
        self.modes = lax.axis_size("mode")
        self.batch = leaves.shape[2]
        self.width = leaves.shape[4]
        self.rows = self.width // self.modes
        self.size = self.modes // self.batch
        self.ways = self.batch
        self.places = self.size // self.ways
        assert self.batch == 2 and lax.axis_size("branch") == 2
        self.steps = [(1, 1), (1, 0), (0, 1), (0, 0)]

    def mode_of(self, high, place, way):
        return (high * self.places + place) * self.ways + way

    def here(self):
        mode = lax.axis_index("mode")
        return mode // self.size, (mode % self.size) // self.ways, mode % self.ways


def first_level(plan, leaves, join_order, jobs, limit):
    width, batch, rows, ways = plan.width, plan.batch, plan.rows, plan.ways
    half = width // ways
    chunks = [blocks for _, _, parts in jobs for blocks in parts]
    totals = [sum(parts) * rows for _, _, parts in jobs]

    def body(order, leaf, *rest):
        outs, rest = rest[: 2 * len(chunks)], rest[2 * len(chunks) :]
        copies = Copies(rest[-1])
        branch = lax.axis_index("branch")
        _, _, way = plan.here()
        loads = []
        for index, (role, begin, parts) in enumerate(jobs):
            upper, lower, _ = rest[3 * index : 3 * index + 3]
            pair = jnp.where(order[2 * lax.axis_size("branch") + branch] == 1, 1 - role, role)
            swapped = jnp.where(order[2 * branch + pair] == 1, 1, 0)
            first, second = 2 * pair + swapped, 2 * pair + 1 - swapped
            for item in range(batch):
                mine = [copies.start(leaf.at[second, :, item], lower.at[item])]
                for side, target in enumerate((way, 1 - way)):
                    span = pl.ds(target * half + begin * rows, totals[index])
                    source = leaf.at[first, :, item, span]
                    mine.append(copies.start(source, upper.at[item, :, side]))
                loads.append(mine)
        stores = []
        given = 0
        for index, (role, begin, parts) in enumerate(jobs):
            upper, lower, result = rest[3 * index : 3 * index + 3]
            total = totals[index]
            for item in range(batch):
                for copy in loads[index * batch + item]:
                    copy.wait()
                sums = complex_dot(
                    upper[item, 0].reshape(ways * total, width),
                    upper[item, 1].reshape(ways * total, width),
                    lower[item].reshape(2 * width, width),
                )
                for part in range(2):
                    result[item, part] = (
                        sums[part].astype(jnp.bfloat16).reshape(ways, total // rows, rows, width)
                    )
                for side in range(ways):
                    done = 0
                    for chunk, blocks in enumerate(parts):
                        source = result.at[item, :, side, pl.ds(done, blocks)]
                        place = outs[2 * (given + chunk) + side].at[:, :, item]
                        stores.append(copies.start(source, place))
                        done += blocks
            given += len(parts)
        for copy in stores:
            copy.wait()

    outs = [
        jax.ShapeDtypeStruct((2, blocks, batch, rows, width), jnp.bfloat16)
        for blocks in chunks
        for _ in range(ways)
    ]
    scratch = []
    for total in totals:
        scratch += [
            pltpu.VMEM((batch, 2, ways, total, width), jnp.bfloat16),
            pltpu.VMEM((batch, 2, width, width), jnp.bfloat16),
            pltpu.VMEM((batch, 2, ways, total // rows, rows, width), jnp.bfloat16),
        ]
    copies = len(jobs) * batch * (1 + ways) + batch * ways * len(chunks)
    flops = 8 * batch * ways * sum(totals) * width**2
    results = run_kernel(
        body, outs, scratch, copies, flops, [join_order, leaves], [SMEM, ANY], limit=limit
    )
    return [results[2 * index : 2 * index + 2] for index in range(len(chunks))]


def once_there(value, after):
    def body(*refs):
        pass

    return pl.pallas_call(
        body,
        out_shape=jax.ShapeDtypeStruct(value.shape, value.dtype),
        in_specs=[ANY] * (1 + len(after)),
        out_specs=ANY,
        input_output_aliases={0: 0},
        compiler_params=pltpu.CompilerParams(vmem_limit_bytes=2**20),
    )(value, *after)


def arrival(after, micros):
    def body(*refs):
        refs[-1][...] = jnp.zeros((8, 128), jnp.float32)

    return pl.pallas_call(
        body,
        out_shape=jax.ShapeDtypeStruct((8, 128), jnp.float32),
        in_specs=[ANY] * len(after),
        out_specs=VMEM,
        compiler_params=pltpu.CompilerParams(vmem_limit_bytes=2**20),
        cost_estimate=pl.CostEstimate(
            flops=micros * 10**9, bytes_accessed=micros * 3 * 10**6, transcendentals=0
        ),
    )(*after)


def second_level(plan, blocks, operands, pick, direct, near):
    width, batch, rows, ways, places = plan.width, plan.batch, plan.rows, plan.ways, plan.places
    held = ways * batch * rows

    def body(*refs):
        left_kept, left_sent, right_kept, right_sent, others = pick(refs[: len(operands)])
        rest = refs[len(operands) :]
        outs, (left, right, result, sems) = rest[:-4], rest[-4:]
        copies = Copies(sems)
        branch = lax.axis_index("branch")
        high, place, way = plan.here()
        loads = []
        for block in range(blocks):
            moves = [
                (right_kept(block), right.at[:, block, place, way]),
                (right_sent(block), right.at[:, block, place, 1 - way]),
                (left_kept(block), left.at[:, block, way]),
                (left_sent(block), left.at[:, block, 1 - way]),
            ]
            for step, (kept, sent) in enumerate(others):
                other = place ^ (step + 1)
                moves.append((kept(block), right.at[:, block, other, way]))
                moves.append((sent(block), right.at[:, block, other, 1 - way]))
            if near:
                for source, target in moves:
                    target[...] = source[...]
            else:
                loads.append([copies.start(source, target) for source, target in moves])
        stores = []
        for block in range(blocks):
            for copy in loads[block] if loads else []:
                copy.wait()
            halves = [
                jnp.concatenate([left[part, block, high ^ a, branch ^ b] for a, b in plan.steps], axis=0)
                for part in range(2)
            ]
            parts = complex_dot(
                halves[0],
                halves[1],
                jnp.concatenate(
                    [right[part, block].reshape(width, width) for part in range(2)], axis=0
                ),
            )
            for part in range(2):
                done = parts[part].astype(jnp.bfloat16).reshape(ways * batch, rows, width)
                if direct:
                    for index in range(ways * batch):
                        outs[index][part, block] = done[index]
                else:
                    result[block, part] = done
            if not direct:
                for index in range(ways * batch):
                    source = result.at[block, :, index]
                    stores.append(copies.start(source, outs[index].at[:, block]))
        for copy in stores:
            copy.wait()

    outs = [jax.ShapeDtypeStruct((2, blocks, rows, width), jnp.bfloat16)] * (ways * batch)
    scratch = [
        pltpu.VMEM((2, blocks, ways, batch, rows, width), jnp.bfloat16),
        pltpu.VMEM((2, blocks, places, ways, batch, rows, width), jnp.bfloat16),
        pltpu.VMEM((blocks, 2, ways * batch, rows, width), jnp.bfloat16),
    ]
    copies = blocks * (2 + 2 * places + ways * batch)
    flops = 8 * blocks * held * width * width
    count = 2 + 2 * places if near else 0
    specs = [VMEM] * count + [ANY] * (len(operands) - count)
    return run_kernel(
        body, outs, scratch, copies, flops, operands, specs, place=VMEM if direct else ANY
    )


def place_operands(plan, order, messages, chunk_blocks, scratch):
    mode = lax.axis_index("mode")
    near, item = (mode // plan.batch) % plan.ways, mode % plan.batch
    top = jnp.where(order[order.shape[0] - 1] == 1, 1, 0)
    begin = 0
    for chunk, blocks in zip(messages, chunk_blocks):
        for (a, b), message in zip(plan.steps, chunk):
            scratch[item ^ b ^ top, :, pl.ds(begin, blocks), near ^ a] = message[...]
        begin += blocks


def top_operands(plan, scratch, half):
    width = plan.width
    kept = plan.size // 2
    left = [
        scratch[0, part, pl.ds(half * kept, kept)].reshape(width // 2, width) for part in range(2)
    ]
    right = jnp.concatenate([scratch[1, part].reshape(width, width) for part in range(2)], axis=0)
    return left[0], left[1], right


def top_scratch(plan):
    return pltpu.VMEM((2, 2, plan.size, plan.batch, plan.rows, plan.width), jnp.bfloat16)


def top_half(plan, join_order, messages, own):
    flat = [message for chunk in messages for message in chunk]
    count = len(messages[0])
    chunk_blocks = [chunk[0].shape[1] for chunk in messages]
    half_shape = (2, plan.width // 2, plan.width)

    def body(order, *refs):
        sources, (out, operands, _) = refs[: len(flat)], refs[len(flat) :]
        core = lax.axis_index("branch")
        grouped = [sources[i : i + count] for i in range(0, len(flat), count)]
        place_operands(plan, order, grouped, chunk_blocks, operands)
        parts = complex_dot(*top_operands(plan, operands, core if own else 1 - core))
        for part in range(2):
            out[part] = parts[part].astype(jnp.bfloat16)

    return run_kernel(
        body,
        [jax.ShapeDtypeStruct(half_shape, jnp.bfloat16)],
        [top_scratch(plan)],
        1,
        4 * plan.width**3,
        [join_order, *flat],
        [SMEM] + [VMEM] * len(flat),
        place=VMEM,
    )[0]


def boundary_products(plan, slice_values, boundary, top_own, top_received):
    width = plan.width
    shape = (2, plan.batch, width // 2, width)

    def body(values, bound, own, received, out, result, sems):
        copies = Copies(sems)
        core = lax.axis_index("branch")
        stores = []
        half = width // 4
        for index, (top, item) in enumerate(((own, core), (received, 1 - core))):
            value = jnp.where(values[item] == 1, 1, 0)
            chosen = bound[value].reshape(2 * width, width)
            for low in range(0, width // 2, half):
                span = pl.ds(low, half)
                parts = complex_dot(top[0, span], top[1, span], chosen)
                for part in range(2):
                    result[index, part, span] = parts[part]
                stores.append(copies.start(result.at[index, :, span], out.at[:, item, span]))
        for copy in stores:
            copy.wait()

    return run_kernel(
        body,
        [jax.ShapeDtypeStruct(shape, jnp.float32)],
        [pltpu.VMEM((plan.batch, 2, width // 2, width), jnp.float32)],
        2 * plan.batch,
        8 * width**3,
        [slice_values, boundary, top_own, top_received],
        [SMEM, VMEM, VMEM, VMEM],
    )[0]


def per_device(leaves, join_order, slice_values, boundary):
    plan = Plan(leaves)
    modes, ways, places, batch = plan.modes, plan.ways, plan.places, plan.batch
    every = [
        (high, place, way)
        for high in range(batch)
        for place in range(places)
        for way in range(ways)
    ]
    over_ways = [(plan.mode_of(h, p, w), plan.mode_of(h, p, w ^ 1)) for h, p, w in every]

    def over_places(step):
        return [(plan.mode_of(h, p, w), plan.mode_of(h, p ^ step, w)) for h, p, w in every]

    def to_rows(a, b):
        pairs = []
        for h, p, w in every:
            for k in range(2):
                target = (p * ways + (h ^ a)) * batch + (k ^ b)
                pairs.append((plan.mode_of(h, p, w) * 2 + k, target * 2 + w))
        return pairs

    quarter = plan.size // 4
    parts = [2 * quarter, 2 * quarter]
    pieces = [[2 * quarter], [quarter, quarter]]
    right = first_level(plan, leaves, join_order, [(1, 0, parts[:1])], VMEM_MOST)
    rest = first_level(plan, leaves, join_order, [(0, 0, parts), (1, parts[0], parts[1:])], VMEM_LIMIT)
    left, right = rest[: len(parts)], right + rest[len(parts) :]
    others = range(1, places)
    messages = []
    for chunk in range(len(parts)):
        left_kept, left_send = left[chunk]
        right_kept, right_send = right[chunk]
        right_sent = lax.ppermute(right_send, "mode", over_ways)
        kept_there = [lax.ppermute(right_kept, "mode", over_places(step)) for step in others]
        left_sent = lax.ppermute(left_send, "mode", over_ways)
        lows = [sum(pieces[chunk][:piece]) for piece in range(len(pieces[chunk]))]
        forward = [right_sent]
        if chunk:
            forward = [
                right_sent[:, low : low + count] for low, count in zip(lows, pieces[chunk])
            ]
            forward[1:] = [once_there(value, [messages[-1][0]]) for value in forward[1:]]
        sent_there = [
            [lax.ppermute(value, "mode", over_places(step)) for step in others]
            for value in forward
        ]
        for piece, (low, count) in enumerate(zip(lows, pieces[chunk])):
            extra = []
            if chunk and piece == 0:
                extra = [messages[-1][2], arrival([*messages[-1][:2], kept_there[0]], 5)]
            elif piece:
                extra = [messages[-2][3]]
            operands = [left_kept, left_sent, right_kept, right_sent]
            operands += [*kept_there, *sent_there[piece], *extra]

            def pick(refs, low=low):
                def by(ref, base):
                    return lambda block: ref.at[:, base + block]

                there = refs[4 : 2 + 2 * places]
                kept, sent = there[: places - 1], there[places - 1 :]
                pairs = [(by(one, low), by(two, 0)) for one, two in zip(kept, sent)]
                return *[by(ref, low) for ref in refs[:4]], pairs

            rows = second_level(plan, count, operands, pick, chunk > 0, True)
            messages.append(
                [
                    lax.ppermute(value, ("mode", "branch"), to_rows(a, b))
                    for value, (a, b) in zip(rows, plan.steps)
                ]
            )
    top_other = top_half(plan, join_order, messages, False)
    top_received = lax.ppermute(top_other, "branch", [(0, 1), (1, 0)])
    top_own = top_half(plan, join_order, messages, True)
    return boundary_products(plan, slice_values, boundary, top_own, top_received)


def solution(mesh):
    in_specs = (P("branch", None, ("cuts", "mode"), None, None), P(), P(("cuts", "mode")), P())
    out_specs = P(None, ("cuts", "mode"), "branch", None)
    return jax.shard_map(
        per_device, mesh=mesh, in_specs=in_specs, out_specs=out_specs, check_vma=False
    )
```
